32 devices in a mesh: member: 4 (over z), dp: 8 (over y, x, core).
Axes of the slice: x: 2, y: 2, z: 4, core: 2. Of those that a mesh axis runs over, the one named last changes fastest.
Arguments:
- latents: bfloat16 [4, 32, 16, 16, 640], P('member', 'dp'), may hold values from -6 to 6
- cotangent: bfloat16 [4, 32, 16, 16, 640], P('member', 'dp'), may hold values from -6 to 6
- weights: float32 [4, 640, 5760], P('member', 'dp'), may hold values from -6 to 6
- first_moment: float32 [4, 640, 5760], P('member', 'dp'), may hold values from -1.2 to 1.2
- second_moment: float32 [4, 640, 5760], P('member', 'dp'), may hold values from 0.02 to 0.5
- sources: int32 [4], replicated, may hold values from 0 to 3, as said below
Outputs:
- latent_grad: bfloat16 [4, 32, 16, 16, 640], P('member', 'dp')
- new_weights: float32 [4, 640, 5760], P('member', 'dp')
- new_first: float32 [4, 640, 5760], P('member', 'dp')
- new_second: float32 [4, 640, 5760], P('member', 'dp')
The draws below stay inside these ranges and needn't reach their ends.
Inputs may be any that keep to these rules, and one draw needn't show every extreme that they name: sources[k] = k for every member that takes no copy; a member that takes a copy names a member that names itself; at most one quarter of the members (at least one) take copies, and at most one quarter (at least one) are named by others.
All inputs are finite; a program needn't handle non-finite values.
Results may differ from the reference program's by a relative error of at most 0.006.
Values may be sent and summed in bfloat16 or wider, within the bound.
A program may use at most 128 MiB of HBM per device.

```python
import math
import jax
import jax.numpy as jnp
from jax import lax

CH_IN = 640
CH_OUT = 640
CROP = 16
IMG_DEV = 4
ADAM_STEP = 10
MEMBERS = 4
BATCH = 32
N_DP = 8


def draw_sources(key, part):
    rank_of = jax.random.permutation(jax.random.fold_in(key, 7), MEMBERS)
    by_rank = jnp.argsort(rank_of, stable=True)
    quarter = max(MEMBERS // 4, 1)
    chosen = jax.random.randint(jax.random.fold_in(key, 11), (MEMBERS,), 0, quarter)
    losing = rank_of >= MEMBERS - quarter
    return jnp.where(losing, by_rank[chosen], jnp.arange(MEMBERS)).astype(jnp.int32)


def levels(stream_key, extent, split, least, high):
    level = 1.0
    for axis_at, shards_of in split:
        steps = jax.random.uniform(jax.random.fold_in(jax.random.fold_in(stream_key, 6), axis_at), (shards_of,), jnp.float32, least / len(split), high / len(split))
        level = level * jnp.repeat(jnp.exp(steps), extent[axis_at] // shards_of).reshape((-1,) + (1,) * (len(extent) - 1 - axis_at))
    return level


def normal_values(stream_key, dims, deviation, limit, pieces=(), kind=jnp.bfloat16):
    drawn = jax.random.normal(stream_key, dims, jnp.float32) * deviation
    if len(pieces) > 0:
        drawn = levels(stream_key, dims, pieces, -0.22, 0.18) * drawn
    return jnp.clip(drawn, min=-limit, max=limit).astype(kind)


def setup_inputs(seed: int = 0) -> dict:
    arg_keys = jax.random.split(jax.random.key(seed), 7)
    return {
        "latents": normal_values(arg_keys[0], (MEMBERS, BATCH, CROP, CROP, CH_IN), 1.0, 6.0, ((0, 4), (1, 8))),
        "cotangent": normal_values(arg_keys[1], (MEMBERS, BATCH, CROP, CROP, CH_OUT), 1.0, 6.0, ((0, 4), (1, 8))),
        "weights": normal_values(arg_keys[2], (MEMBERS, CH_IN, 9 * CH_OUT), 1.0, 6.0, ((0, 4), (1, 8)), jnp.float32),
        "first_moment": normal_values(arg_keys[3], (MEMBERS, CH_IN, 9 * CH_OUT), 0.2, 1.2, ((0, 4), (1, 8)), jnp.float32),
        "second_moment": jnp.clip(jnp.exp(math.log(0.5) - 3.218876 * jax.random.uniform(arg_keys[4], (MEMBERS, CH_IN, 9 * CH_OUT), jnp.float32) ** levels(arg_keys[4], (MEMBERS, CH_IN, 9 * CH_OUT), ((0, 4), (1, 8)), -0.2, 0.2)), 0.02, 0.5),
        "sources": draw_sources(jax.random.fold_in(arg_keys[6], 71), 0),
    }


BETA_ONE = 0.9
BETA_TWO = 0.99
RATE = 0.05
EPSILON = 1e-08

def silu_slope(values):
    sig = jax.nn.sigmoid(values)
    return sig * (1.0 + values * (1.0 - sig))

def forward_taps(activation, kernel_bf):
    side_cells = activation.shape[1]
    cell_count = activation.shape[0] * side_cells * side_cells
    cols_out = kernel_bf.shape[1] // 9
    padded = jnp.pad(activation, ((0, 0), (1, 1), (1, 1), (0, 0)))
    summed = jnp.zeros((cell_count, cols_out), jnp.float32)
    for tap_index in range(9):
        tap_row = tap_index // 3
        tap_col = tap_index % 3
        window = padded[:, tap_row:tap_row + side_cells, tap_col:tap_col + side_cells, :].reshape(cell_count, activation.shape[3])
        summed = summed + jnp.dot(window, kernel_bf[:, tap_index * cols_out:(tap_index + 1) * cols_out], preferred_element_type=jnp.float32)
    return summed

def backward_taps(deltas, kernel_bf):
    side_cells = deltas.shape[1]
    cell_count = deltas.shape[0] * side_cells * side_cells
    cols_out = deltas.shape[3]
    padded = jnp.pad(deltas, ((0, 0), (1, 1), (1, 1), (0, 0)))
    summed = jnp.zeros((cell_count, kernel_bf.shape[0]), jnp.float32)
    for tap_index in range(9):
        tap_row = tap_index // 3
        tap_col = tap_index % 3
        window = padded[:, 2 - tap_row:2 - tap_row + side_cells, 2 - tap_col:2 - tap_col + side_cells, :].reshape(cell_count, cols_out)
        block = kernel_bf[:, tap_index * cols_out:(tap_index + 1) * cols_out]
        summed = summed + lax.dot_general(window, block, (((1,), (1,)), ((), ())), preferred_element_type=jnp.float32)
    return summed

def weight_taps(activation, deltas):
    side_cells = activation.shape[1]
    cell_count = activation.shape[0] * side_cells * side_cells
    flat_deltas = deltas.reshape(cell_count, deltas.shape[3])
    padded = jnp.pad(activation, ((0, 0), (1, 1), (1, 1), (0, 0)))
    blocks = []
    for tap_index in range(9):
        tap_row = tap_index // 3
        tap_col = tap_index % 3
        window = padded[:, tap_row:tap_row + side_cells, tap_col:tap_col + side_cells, :].reshape(cell_count, activation.shape[3])
        blocks.append(lax.dot_general(window, flat_deltas, (((0,), (0,)), ((), ())), preferred_element_type=jnp.float32))
    return jnp.concatenate(blocks, axis=1)

def adam_update(weights_now, first_now, second_now, gradient):
    first_new = BETA_ONE * first_now + (1.0 - BETA_ONE) * gradient
    second_new = BETA_TWO * second_now + (1.0 - BETA_TWO) * gradient * gradient
    first_fix = 1.0 - BETA_ONE ** ADAM_STEP
    second_fix = 1.0 - BETA_TWO ** ADAM_STEP
    updated = weights_now - RATE * (first_new / first_fix) / (jnp.sqrt(second_new / second_fix) + EPSILON)
    return (updated, first_new, second_new)

def member_step(inputs):
    latents_one, cotangent_one, weights_one, first_one, second_one = inputs
    scale = (9 * CH_IN) ** (-0.5)
    activation = jax.nn.silu(latents_one.astype(jnp.float32)).astype(jnp.bfloat16)
    kernel_bf = weights_one.astype(jnp.bfloat16)
    hidden = scale * forward_taps(activation, kernel_bf)
    cell_count = hidden.shape[0]
    deltas = (cotangent_one.reshape(cell_count, CH_OUT).astype(jnp.float32) * silu_slope(hidden)).astype(jnp.bfloat16)
    deltas_img = deltas.reshape(cotangent_one.shape)
    back = scale * backward_taps(deltas_img, kernel_bf)
    slope_in = silu_slope(latents_one.reshape(cell_count, CH_IN).astype(jnp.float32))
    latent_grad = (back * slope_in).astype(jnp.bfloat16).reshape(latents_one.shape)
    act_blocks = activation.reshape((N_DP, IMG_DEV) + activation.shape[1:])
    delta_blocks = deltas_img.reshape((N_DP, IMG_DEV) + deltas_img.shape[1:])

    def accumulate(carry, pair):
        part = (scale * weight_taps(pair[0], pair[1])).astype(jnp.bfloat16)
        part = lax.optimization_barrier(part)
        return (carry + part.astype(jnp.float32), None)
    start_sum = jnp.zeros((CH_IN, 9 * CH_OUT), jnp.float32)
    gradient, _ = lax.scan(accumulate, start_sum, (act_blocks, delta_blocks))
    updated, first_new, second_new = adam_update(weights_one, first_one, second_one, gradient)
    return (latent_grad, updated, first_new, second_new)

def reference(latents, cotangent, weights, first_moment, second_moment, sources):
    latent_grad, updated, first_new, second_new = lax.map(member_step, (latents, cotangent, weights, first_moment, second_moment))
    picks = sources.astype(jnp.int32)
    new_weights = jnp.take(updated, picks, axis=0)
    new_first = jnp.take(first_new, picks, axis=0)
    new_second = jnp.take(second_new, picks, axis=0)
    return (latent_grad, new_weights, new_first, new_second)
```

```python
import jax
import jax.numpy as jnp
from jax import lax
from jax.sharding import PartitionSpec as P

CH_IN = 640
ADAM_STEP = 10


BETA_ONE = 0.9
BETA_TWO = 0.99
RATE = 0.05
EPSILON = 1e-08


def silu_slope(values):
    sig = jax.nn.sigmoid(values)
    return sig * (1.0 + values * (1.0 - sig))


def forward_taps(activation, kernel_bf):
    side_cells = activation.shape[1]
    cell_count = activation.shape[0] * side_cells * side_cells
    cols_out = kernel_bf.shape[1] // 9
    padded = jnp.pad(activation, ((0, 0), (1, 1), (1, 1), (0, 0)))
    summed = jnp.zeros((cell_count, cols_out), jnp.float32)
    for tap_index in range(9):
        tap_row = tap_index // 3
        tap_col = tap_index % 3
        window = padded[
            :, tap_row : tap_row + side_cells, tap_col : tap_col + side_cells, :
        ].reshape(cell_count, activation.shape[3])
        summed = summed + jnp.dot(
            window,
            kernel_bf[:, tap_index * cols_out : (tap_index + 1) * cols_out],
            preferred_element_type=jnp.float32,
        )
    return summed


def backward_taps(deltas, kernel_bf):
    side_cells = deltas.shape[1]
    cell_count = deltas.shape[0] * side_cells * side_cells
    cols_out = deltas.shape[3]
    padded = jnp.pad(deltas, ((0, 0), (1, 1), (1, 1), (0, 0)))
    summed = jnp.zeros((cell_count, kernel_bf.shape[0]), jnp.float32)
    for tap_index in range(9):
        tap_row = tap_index // 3
        tap_col = tap_index % 3
        window = padded[
            :, 2 - tap_row : 2 - tap_row + side_cells, 2 - tap_col : 2 - tap_col + side_cells, :
        ].reshape(cell_count, cols_out)
        block = kernel_bf[:, tap_index * cols_out : (tap_index + 1) * cols_out]
        summed = summed + lax.dot_general(
            window, block, (((1,), (1,)), ((), ())), preferred_element_type=jnp.float32
        )
    return summed


def weight_taps(activation, deltas):
    side_cells = activation.shape[1]
    cell_count = activation.shape[0] * side_cells * side_cells
    flat_deltas = deltas.reshape(cell_count, deltas.shape[3])
    padded = jnp.pad(activation, ((0, 0), (1, 1), (1, 1), (0, 0)))
    blocks = []
    for tap_index in range(9):
        tap_row = tap_index // 3
        tap_col = tap_index % 3
        window = padded[
            :, tap_row : tap_row + side_cells, tap_col : tap_col + side_cells, :
        ].reshape(cell_count, activation.shape[3])
        blocks.append(
            lax.dot_general(
                window, flat_deltas, (((0,), (0,)), ((), ())), preferred_element_type=jnp.float32
            )
        )
    return jnp.concatenate(blocks, axis=1)


def adam_update(weights_now, first_now, second_now, gradient):
    first_new = BETA_ONE * first_now + (1.0 - BETA_ONE) * gradient
    second_new = BETA_TWO * second_now + (1.0 - BETA_TWO) * gradient * gradient
    first_fix = 1.0 - BETA_ONE**ADAM_STEP
    second_fix = 1.0 - BETA_TWO**ADAM_STEP
    updated = weights_now - RATE * (first_new / first_fix) / (
        jnp.sqrt(second_new / second_fix) + EPSILON
    )
    return (updated, first_new, second_new)


def takers_and_named(sources):
    members = sources.shape[0]
    slots = max(members // 4, 1)
    own = jnp.arange(members, dtype=jnp.int32)
    takers = jnp.argsort(jnp.where(sources == own, 1, 0), stable=True)[:slots]
    return takers, sources[takers]


def carry_over(stacked, takers, named):
    me = lax.axis_index("member")
    sent = [
        jnp.where(named[slot] == me, stacked, jnp.zeros_like(stacked))
        for slot in range(takers.shape[0])
    ]
    arrived = lax.psum(jnp.stack(sent), "member")
    return arrived


def local(latents, cotangent, weights, first_moment, second_moment, sources):
    scale = (9 * CH_IN) ** (-0.5)
    me = lax.axis_index("member")
    takers, named = takers_and_named(sources)
    images = latents[0]
    activation = jax.nn.silu(images.astype(jnp.float32)).astype(jnp.bfloat16)
    kernel_rows = weights[0].astype(jnp.bfloat16)
    state = jnp.concatenate(
        [kernel_rows, first_moment[0].astype(jnp.bfloat16), second_moment[0].astype(jnp.bfloat16)]
    )
    cell_count = images.shape[0] * images.shape[1] * images.shape[2]
    cols_out = cotangent.shape[4]
    kernel_all = lax.all_gather(kernel_rows, "dp", axis=0, tiled=True)
    arrived = carry_over(state, takers, named)
    hidden = scale * forward_taps(activation, kernel_all)
    deltas = (
        cotangent[0].reshape(cell_count, cols_out).astype(jnp.float32) * silu_slope(hidden)
    ).astype(jnp.bfloat16)
    deltas_img = deltas.reshape(cotangent[0].shape)
    back = scale * backward_taps(deltas_img, kernel_all)
    slope_in = silu_slope(images.reshape(cell_count, images.shape[3]).astype(jnp.float32))
    latent_grad = (back * slope_in).astype(jnp.bfloat16).reshape(latents.shape)
    gradient = lax.psum_scatter(
        (scale * weight_taps(activation, deltas_img)).astype(jnp.bfloat16),
        "dp",
        scatter_dimension=0,
        tiled=True,
    )
    gradient, arrived = lax.optimization_barrier((gradient, arrived))
    moved_gradient = carry_over(gradient, takers, named)
    rows = gradient.shape[0]
    weights_now, first_now, second_now = weights[0], first_moment[0], second_moment[0]
    gradient = gradient.astype(jnp.float32)
    for slot in range(takers.shape[0]):
        taking = (takers[slot] == me) & (named[slot] != me)
        moved = arrived[slot].astype(jnp.float32)
        weights_now = jnp.where(taking, moved[:rows], weights_now)
        first_now = jnp.where(taking, moved[rows : 2 * rows], first_now)
        second_now = jnp.where(taking, moved[2 * rows :], second_now)
        gradient = jnp.where(taking, moved_gradient[slot].astype(jnp.float32), gradient)
    updated, first_new, second_new = adam_update(weights_now, first_now, second_now, gradient)
    return (latent_grad, updated[None], first_new[None], second_new[None])


def solution(mesh):
    in_specs = (
        P("member", "dp", None, None, None),
        P("member", "dp", None, None, None),
        P("member", "dp", None),
        P("member", "dp", None),
        P("member", "dp", None),
        P(),
    )
    out_specs = (
        P("member", "dp", None, None, None),
        P("member", "dp", None),
        P("member", "dp", None),
        P("member", "dp", None),
    )
    return jax.shard_map(local, mesh=mesh, in_specs=in_specs, out_specs=out_specs, check_vma=False)
```

```python
import jax
import jax.numpy as jnp
from jax import lax
from jax.experimental import pallas as pl
from jax.experimental.pallas import tpu as pltpu
from jax.sharding import PartitionSpec as P

CH_IN = 640
ADAM_STEP = 10


BETA_ONE = 0.9
BETA_TWO = 0.99
RATE = 0.05
EPSILON = 1e-08


def silu_slope(values):
    sig = jax.nn.sigmoid(values)
    return sig * (1.0 + values * (1.0 - sig))


def forward_taps(activation, kernel_bf):
    side_cells = activation.shape[1]
    cell_count = activation.shape[0] * side_cells * side_cells
    cols_out = kernel_bf.shape[1] // 9
    padded = jnp.pad(activation, ((0, 0), (1, 1), (1, 1), (0, 0)))
    summed = jnp.zeros((cell_count, cols_out), jnp.float32)
    for tap_index in range(9):
        tap_row = tap_index // 3
        tap_col = tap_index % 3
        window = padded[
            :, tap_row : tap_row + side_cells, tap_col : tap_col + side_cells, :
        ].reshape(cell_count, activation.shape[3])
        summed = summed + jnp.dot(
            window,
            kernel_bf[:, tap_index * cols_out : (tap_index + 1) * cols_out],
            preferred_element_type=jnp.float32,
        )
    return summed


def backward_taps(deltas, kernel_bf):
    side_cells = deltas.shape[1]
    cell_count = deltas.shape[0] * side_cells * side_cells
    cols_out = deltas.shape[3]
    padded = jnp.pad(deltas, ((0, 0), (1, 1), (1, 1), (0, 0)))
    summed = jnp.zeros((cell_count, kernel_bf.shape[0]), jnp.float32)
    for tap_index in range(9):
        tap_row = tap_index // 3
        tap_col = tap_index % 3
        window = padded[
            :, 2 - tap_row : 2 - tap_row + side_cells, 2 - tap_col : 2 - tap_col + side_cells, :
        ].reshape(cell_count, cols_out)
        block = kernel_bf[:, tap_index * cols_out : (tap_index + 1) * cols_out]
        summed = summed + lax.dot_general(
            window, block, (((1,), (1,)), ((), ())), preferred_element_type=jnp.float32
        )
    return summed


def weight_taps(activation, deltas):
    side_cells = activation.shape[1]
    cell_count = activation.shape[0] * side_cells * side_cells
    flat_deltas = deltas.reshape(cell_count, deltas.shape[3])
    padded = jnp.pad(activation, ((0, 0), (1, 1), (1, 1), (0, 0)))
    blocks = []
    for tap_index in range(9):
        tap_row = tap_index // 3
        tap_col = tap_index % 3
        window = padded[
            :, tap_row : tap_row + side_cells, tap_col : tap_col + side_cells, :
        ].reshape(cell_count, activation.shape[3])
        blocks.append(
            lax.dot_general(
                window, flat_deltas, (((0,), (0,)), ((), ())), preferred_element_type=jnp.float32
            )
        )
    return jnp.concatenate(blocks, axis=1)


def adam_update(weights_now, first_now, second_now, gradient):
    first_new = BETA_ONE * first_now + (1.0 - BETA_ONE) * gradient
    second_new = BETA_TWO * second_now + (1.0 - BETA_TWO) * gradient * gradient
    first_fix = 1.0 - BETA_ONE**ADAM_STEP
    second_fix = 1.0 - BETA_TWO**ADAM_STEP
    updated = weights_now - RATE * (first_new / first_fix) / (
        jnp.sqrt(second_new / second_fix) + EPSILON
    )
    return (updated, first_new, second_new)


def takers_and_named(sources):
    members = sources.shape[0]
    slots = max(members // 4, 1)
    own = jnp.arange(members, dtype=jnp.int32)
    takers = jnp.argsort(jnp.where(sources == own, 1, 0), stable=True)[:slots]
    return takers, sources[takers]


def carry_over(stacked, takers, named):
    me = lax.axis_index("member")
    sent = [
        jnp.where(named[slot] == me, stacked, jnp.zeros_like(stacked))
        for slot in range(takers.shape[0])
    ]
    arrived = lax.psum(jnp.stack(sent), "member")
    return arrived


def local_plain(latents, cotangent, weights, first_moment, second_moment, sources):
    scale = (9 * CH_IN) ** (-0.5)
    me = lax.axis_index("member")
    takers, named = takers_and_named(sources)
    images = latents[0]
    activation = jax.nn.silu(images.astype(jnp.float32)).astype(jnp.bfloat16)
    kernel_rows = weights[0].astype(jnp.bfloat16)
    state = jnp.concatenate(
        [kernel_rows, first_moment[0].astype(jnp.bfloat16), second_moment[0].astype(jnp.bfloat16)]
    )
    cell_count = images.shape[0] * images.shape[1] * images.shape[2]
    cols_out = cotangent.shape[4]
    kernel_all = lax.all_gather(kernel_rows, "dp", axis=0, tiled=True)
    arrived = carry_over(state, takers, named)
    hidden = scale * forward_taps(activation, kernel_all)
    deltas = (
        cotangent[0].reshape(cell_count, cols_out).astype(jnp.float32) * silu_slope(hidden)
    ).astype(jnp.bfloat16)
    deltas_img = deltas.reshape(cotangent[0].shape)
    back = scale * backward_taps(deltas_img, kernel_all)
    slope_in = silu_slope(images.reshape(cell_count, images.shape[3]).astype(jnp.float32))
    latent_grad = (back * slope_in).astype(jnp.bfloat16).reshape(latents.shape)
    gradient = lax.psum_scatter(
        (scale * weight_taps(activation, deltas_img)).astype(jnp.bfloat16),
        "dp",
        scatter_dimension=0,
        tiled=True,
    )
    gradient, arrived = lax.optimization_barrier((gradient, arrived))
    moved_gradient = carry_over(gradient, takers, named)
    rows = gradient.shape[0]
    weights_now, first_now, second_now = weights[0], first_moment[0], second_moment[0]
    gradient = gradient.astype(jnp.float32)
    for slot in range(takers.shape[0]):
        taking = (takers[slot] == me) & (named[slot] != me)
        moved = arrived[slot].astype(jnp.float32)
        weights_now = jnp.where(taking, moved[:rows], weights_now)
        first_now = jnp.where(taking, moved[rows : 2 * rows], first_now)
        second_now = jnp.where(taking, moved[2 * rows :], second_now)
        gradient = jnp.where(taking, moved_gradient[slot].astype(jnp.float32), gradient)
    updated, first_new, second_new = adam_update(weights_now, first_now, second_now, gradient)
    return (latent_grad, updated[None], first_new[None], second_new[None])


HALF = 48


def shifted(values):
    none = jnp.zeros((1, values.shape[1]), jnp.float32)
    before = jnp.concatenate([none, values[:-1]], axis=0)
    after = jnp.concatenate([values[1:], none], axis=0)
    return before, values, after


def block_kernel(
    flags,
    latents,
    cotangent,
    state,
    latent_grad,
    grad,
    arrived,
    moved,
    kall,
    near,
    act_t,
    total,
    partial,
    core_in,
    chip_sum,
    x_in,
    y_in,
    a_sum,
    b_sum,
    a_in,
    b_in,
    up_in,
    down_in,
    up_grad,
    down_grad,
    ag_send,
    ag_recv,
    rs_send,
    rs_recv,
    z_send,
    z_recv,
):
    images, side = latents.shape[0], latents.shape[1]
    width = latents.shape[3]
    cells = side * side
    rows = state.shape[2]
    scale = (9 * CH_IN) ** (-0.5)
    f32, bf16 = jnp.float32, jnp.bfloat16
    k = lax.axis_index("member")
    me = lax.axis_index("dp")
    y, x, c = me // 4, (me // 2) % 2, me % 2
    sib = me + 1 - 2 * c
    xp = me + 2 - 4 * x
    yp = me + 4 - 8 * y
    diag = xp + 4 - 8 * y
    named = flags[0]
    from_below = flags[1]

    def remote(src, dst, send, recv, member, index):
        return pltpu.make_async_remote_copy(
            src_ref=src,
            dst_ref=dst,
            send_sem=send,
            recv_sem=recv,
            device_id=(member, index),
            device_id_type=pl.DeviceIdType.MESH,
        )

    barrier = pltpu.get_barrier_semaphore()
    for peer in (sib, xp, yp):
        pl.semaphore_signal(
            barrier, inc=1, device_id=(k, peer), device_id_type=pl.DeviceIdType.MESH
        )

    @pl.when(k < 3)
    def _():
        pl.semaphore_signal(
            barrier, inc=1, device_id=(k + 1, me), device_id_type=pl.DeviceIdType.MESH
        )

    @pl.when(k > 0)
    def _():
        pl.semaphore_signal(
            barrier, inc=1, device_id=(k - 1, me), device_id_type=pl.DeviceIdType.MESH
        )

    pl.semaphore_wait(barrier, 3 + jnp.where(k < 3, 1, 0) + jnp.where(k > 0, 1, 0))

    def block(t, owner, first=0, count=rows):
        return kall.at[t, owner, pl.ds(first, count)]

    def gather(t, kind):
        if kind < 3:
            part, peer = block(t, me), (sib, xp, yp)[kind]
        elif kind == 3:
            part, peer = block(t, xp, 0, HALF), yp
        elif kind == 4:
            part, peer = block(t, yp, HALF, rows - HALF), xp
        else:
            part, peer = block(t, (xp, yp, diag)[kind - 5]), sib
        return remote(part, part, ag_send.at[t, kind], ag_recv.at[t, kind], k, peer)

    def gather_wait(t, kind):
        gather_in(t, kind).wait_recv()

    def gather_in(t, kind):
        if kind < 3:
            part = block(t, (sib, xp, yp)[kind])
        elif kind == 3:
            part = block(t, diag, 0, HALF)
        elif kind == 4:
            part = block(t, diag, HALF, rows - HALF)
        else:
            over = 1 - 2 * c
            part = block(t, (xp + over, yp + over, diag + over)[kind - 5])
        return remote(part, part, ag_send.at[t, kind], ag_recv.at[t, kind], k, sib)

    def state_step(tick, lane, rank, here, target):
        j = tick // 2 - 2 * rank

        @pl.when((tick % 2 == 0) & (j >= 0) & (j < 9) & (rank < 3))
        def _():
            @pl.when(rank == 0)
            def _():
                here[j] = state[j]

            @pl.when(rank > 0)
            def _():
                remote(
                    here.at[j], here.at[j], z_send.at[lane, j], z_recv.at[lane, j], target, me
                ).wait_recv()
                mine, came = state[j].astype(f32), here[j].astype(f32)
                here[j] = (mine * named + came * (1.0 - named)).astype(bf16)

            remote(
                here.at[j], here.at[j], z_send.at[lane, j], z_recv.at[lane, j], target, me
            ).start()

    def grad_step(tick, lane, rank, here, target):
        t = tick - 14 - 2 * rank

        @pl.when((t >= 0) & (t < 9) & (rank < 3))
        def _():
            copy = remote(
                here.at[t], here.at[t], z_send.at[lane, t], z_recv.at[lane, t], target, me
            )

            @pl.when(rank == 0)
            def _():
                here[t] = grad[t]

            @pl.when(rank > 0)
            def _():
                copy.wait_recv()
                mine, came = grad[t].astype(f32), here[t].astype(f32)
                here[t] = (mine * named + came * (1.0 - named)).astype(bf16)

            copy.start()

    def member_steps(tick, with_grad):
        state_step(tick, 0, k, up_in, jnp.minimum(k + 1, 3))
        state_step(tick, 1, 3 - k, down_in, jnp.maximum(k - 1, 0))
        if with_grad:
            grad_step(tick, 2, k, up_grad, jnp.minimum(k + 1, 3))
            grad_step(tick, 3, 3 - k, down_grad, jnp.maximum(k - 1, 0))

    def cast_tap(t, carry):
        kall[t, me] = state[t, 0]
        return carry

    lax.fori_loop(0, 9, cast_tap, 0)

    def first_sends(t):
        for kind in range(3):
            gather(t, kind).start()

    def ahead(t, carry):
        first_sends(t)
        return carry

    lax.fori_loop(0, 4, ahead, 0)

    zero_row = jnp.zeros((side, width), bf16)

    def clear(n, carry):
        near[n // images, n % images, 0] = zero_row
        near[n // images, n % images, side + 1] = zero_row
        return carry

    lax.fori_loop(0, 3 * images, clear, 0)

    def activate(n, carry):
        b, i = n // side, n % side
        value = latents[b, i].astype(f32)
        value = value / (1.0 + jnp.exp(-value))
        for at, moved_values in enumerate(shifted(value)):
            near[at, b, i + 1] = moved_values.astype(bf16)
        return carry

    lax.fori_loop(0, images * side, activate, 0)
    for b in range(images):
        flat = near[1, b, 1 : side + 1].reshape(cells, width)
        act_t[:, b * cells : (b + 1) * cells] = jnp.transpose(flat)

    def forward(i, carry):
        @pl.when(i < 9)
        def _():
            member_steps(i, False)

        @pl.when(i + 4 < 9)
        def _():
            first_sends(i + 4)

        @pl.when(i < 9)
        def _():
            gather_wait(i, 1)
            gather_wait(i, 2)
            for kind in (3, 4, 5, 6):
                gather(i, kind).start()

        @pl.when((i >= 1) & (i < 10))
        def _():
            gather_wait(i - 1, 3)
            gather_wait(i - 1, 4)
            gather(i - 1, 7).start()

        @pl.when(i >= 2)
        def _():
            t = i - 2
            for kind in (0, 5, 6, 7):
                gather_wait(t, kind)
            weight = kall[t].reshape(8 * rows, width)

            def one(b, carry):
                window = near[t % 3, b, pl.ds(t // 3, side)].reshape(cells, width)
                product = jnp.dot(window, weight, preferred_element_type=f32)
                total[b] = jnp.where(t == 0, 0.0, total[b]) + product
                return carry

            lax.fori_loop(0, images, one, 0)

        return carry

    lax.fori_loop(0, 11, forward, 0)

    def slope_rows(n, carry):
        b, i = n // side, n % side
        hidden = scale * total[b, pl.ds(pl.multiple_of(i * side, side), side)]
        value = cotangent[b, i].astype(f32) * silu_slope(hidden)
        for at, moved_values in enumerate(shifted(value)):
            near[at, b, i + 1] = moved_values.astype(bf16)
        return carry

    lax.fori_loop(0, images * side, slope_rows, 0)

    def window_of(t, b):
        return near[2 - t % 3, b, pl.ds(2 - t // 3, side)].reshape(cells, width)

    def scatter(t, kind):
        if kind == 0:
            src, dst, peer = partial.at[t, :, :, 1 - c], core_in.at[t], sib
        elif kind == 1:
            src, dst, peer = chip_sum.at[t, :, 1 - x, pl.ds(0, HALF)], x_in.at[t], xp
        elif kind == 2:
            src, dst, peer = chip_sum.at[t, 1 - y, :, pl.ds(HALF, rows - HALF)], y_in.at[t], yp
        elif kind == 3:
            src, dst, peer = a_sum.at[t, 1 - y], a_in.at[t], yp
        else:
            src, dst, peer = b_sum.at[t, 1 - x], b_in.at[t], xp
        return remote(src, dst, rs_send.at[t, kind], rs_recv.at[t, kind], k, peer)

    def plus(one, two):
        return (one.astype(f32) + two.astype(f32)).astype(bf16)

    def scatter_steps(i):
        @pl.when((i >= 1) & (i < 10))
        def _():
            t = i - 1
            scatter(t, 0).wait_recv()
            for yy in range(2):
                for xx in range(2):
                    chip_sum[t, yy, xx] = plus(partial[t, yy, xx, c], core_in[t, yy, xx])
            scatter(t, 1).start()
            scatter(t, 2).start()

        @pl.when((i >= 3) & (i < 12))
        def _():
            t = i - 3
            scatter(t, 1).wait_recv()
            scatter(t, 2).wait_recv()
            for at in range(2):
                a_sum[t, at] = plus(chip_sum[t, at, x, 0:HALF], x_in[t, at])
                b_sum[t, at] = plus(chip_sum[t, y, at, HALF:rows], y_in[t, at])
            scatter(t, 3).start()
            scatter(t, 4).start()

        @pl.when((i >= 5) & (i < 14))
        def _():
            t = i - 5
            scatter(t, 3).wait_recv()
            scatter(t, 4).wait_recv()
            grad[t, 0:HALF] = plus(a_sum[t, y], a_in[t])
            grad[t, HALF:rows] = plus(b_sum[t, x], b_in[t])

    def kernel_grad(t, carry):
        scatter_steps(t)
        member_steps(t + 9, True)
        window = near[2 - t % 3, :, pl.ds(2 - t // 3, side)].reshape(images * cells, width)

        def one(yy, carry):
            lhs = act_t[pl.ds(pl.multiple_of(yy * 4 * rows, 64), 4 * rows)]
            product = scale * jnp.dot(lhs, window, preferred_element_type=f32)
            partial[t, yy] = product.astype(bf16).reshape(2, 2, rows, width)
            return carry

        lax.fori_loop(0, 2, one, 0)
        scatter(t, 0).start()
        return carry

    lax.fori_loop(0, 9, kernel_grad, 0)

    def back(t, carry):
        scatter_steps(t + 9)
        member_steps(t + 18, True)
        weight = kall[t].reshape(8 * rows, width)

        def one(b, carry):
            product = lax.dot_general(
                window_of(t, b), weight, (((1,), (1,)), ((), ())), preferred_element_type=f32
            )
            total[b] = jnp.where(t == 0, 0.0, total[b]) + product
            return carry

        lax.fori_loop(0, images, one, 0)
        return carry

    lax.fori_loop(0, 9, back, 0)

    def finish(n, carry):
        b, i = n // side, n % side
        value = scale * total[b, pl.ds(pl.multiple_of(i * side, side), side)]
        value = value * silu_slope(latents[b, i].astype(f32))
        latent_grad[b, i] = value.astype(bf16)
        return carry

    lax.fori_loop(0, images * side, finish, 0)

    def pick(dst, below, above, j):
        @pl.when(k == 0)
        def _():
            dst[j] = above[j]

        @pl.when(k == 3)
        def _():
            dst[j] = below[j]

        @pl.when((k > 0) & (k < 3))
        def _():
            lower, upper = below[j].astype(f32), above[j].astype(f32)
            dst[j] = (lower * from_below + upper * (1.0 - from_below)).astype(bf16)

    def drain(j, carry):
        for lane, here in enumerate((up_in, down_in, up_grad, down_grad)):
            copy = remote(here.at[j], here.at[j], z_send.at[lane, j], z_recv.at[lane, j], k, sib)
            last = k == 3 if lane % 2 == 0 else k == 0

            @pl.when(last)
            def _():
                copy.wait_recv()

            @pl.when(jnp.logical_not(last))
            def _():
                copy.wait_send()

        pick(arrived, up_in, down_in, j)
        pick(moved, up_grad, down_grad, j)
        for kind in range(8):
            gather(j, kind).wait_send()
        for kind in range(5):
            scatter(j, kind).wait_send()
        return carry

    lax.fori_loop(0, 9, drain, 0)


def local_block(latents, cotangent, weights, first_moment, second_moment, sources):
    me = lax.axis_index("member")
    takers, named = takers_and_named(sources)
    taker, source = takers[0], named[0]
    rows, width = weights.shape[1], latents.shape[4]
    bf16 = jnp.bfloat16
    state = jnp.stack([weights[0], first_moment[0], second_moment[0]]).astype(bf16)
    state = state.reshape(3, rows, 9, width).transpose(2, 0, 1, 3)
    flags = jnp.stack([source == me, source < taker]).astype(jnp.float32)
    images, side = latents.shape[1], latents.shape[2]
    cells = side * side
    vmem = pl.BlockSpec(memory_space=pltpu.VMEM)
    tap = (9, rows, width)
    half, rest = HALF, rows - HALF
    latent_grad, grad, arrived, moved = pl.pallas_call(
        block_kernel,
        out_shape=(
            jax.ShapeDtypeStruct(latents.shape[1:], bf16),
            jax.ShapeDtypeStruct(tap, bf16),
            jax.ShapeDtypeStruct((9, 3, rows, width), bf16),
            jax.ShapeDtypeStruct(tap, bf16),
        ),
        in_specs=[pl.BlockSpec(memory_space=pltpu.SMEM), vmem, vmem, vmem],
        out_specs=(vmem,) * 4,
        scratch_shapes=[
            pltpu.VMEM((9, 8, rows, width), bf16),
            pltpu.VMEM((3, images, side + 2, side, width), bf16),
            pltpu.VMEM((width, images * cells), bf16),
            pltpu.VMEM((images, cells, width), jnp.float32),
            pltpu.VMEM((9, 2, 2, 2, rows, width), bf16),
            pltpu.VMEM((9, 2, 2, rows, width), bf16),
            pltpu.VMEM((9, 2, 2, rows, width), bf16),
            pltpu.VMEM((9, 2, half, width), bf16),
            pltpu.VMEM((9, 2, rest, width), bf16),
            pltpu.VMEM((9, 2, half, width), bf16),
            pltpu.VMEM((9, 2, rest, width), bf16),
            pltpu.VMEM((9, half, width), bf16),
            pltpu.VMEM((9, rest, width), bf16),
            pltpu.VMEM((9, 3, rows, width), bf16),
            pltpu.VMEM((9, 3, rows, width), bf16),
            pltpu.VMEM(tap, bf16),
            pltpu.VMEM(tap, bf16),
            pltpu.SemaphoreType.DMA((9, 8)),
            pltpu.SemaphoreType.DMA((9, 8)),
            pltpu.SemaphoreType.DMA((9, 5)),
            pltpu.SemaphoreType.DMA((9, 5)),
            pltpu.SemaphoreType.DMA((4, 9)),
            pltpu.SemaphoreType.DMA((4, 9)),
        ],
        compiler_params=pltpu.CompilerParams(
            collective_id=0, has_side_effects=True, vmem_limit_bytes=60 * 1024 * 1024
        ),
        cost_estimate=pl.CostEstimate(
            flops=6 * images * cells * 9 * width * width, bytes_accessed=16000000, transcendentals=0
        ),
    )(flags, latents[0], cotangent[0], state)

    def flat(taps):
        return taps.astype(jnp.float32).transpose(1, 0, 2).reshape(rows, 9 * width)

    taking = (taker == me) & (source != me)
    weights_now = jnp.where(taking, flat(arrived[:, 0]), weights[0])
    first_now = jnp.where(taking, flat(arrived[:, 1]), first_moment[0])
    second_now = jnp.where(taking, flat(arrived[:, 2]), second_moment[0])
    gradient = flat(jnp.where(taking, moved, grad))
    updated, first_new, second_new = adam_update(weights_now, first_now, second_now, gradient)
    return (latent_grad[None], updated[None], first_new[None], second_new[None])


def solution(mesh):
    fits = mesh.shape["member"] == 4 and mesh.shape["dp"] == 8
    local = local_block if fits else local_plain
    in_specs = (
        P("member", "dp", None, None, None),
        P("member", "dp", None, None, None),
        P("member", "dp", None),
        P("member", "dp", None),
        P("member", "dp", None),
        P(),
    )
    out_specs = (
        P("member", "dp", None, None, None),
        P("member", "dp", None),
        P("member", "dp", None),
        P("member", "dp", None),
    )
    return jax.shard_map(local, mesh=mesh, in_specs=in_specs, out_specs=out_specs, check_vma=False)
```

```python
import jax
import jax.numpy as jnp
from jax import lax
from jax.experimental import pallas as pl
from jax.experimental.pallas import tpu as pltpu
from jax.sharding import PartitionSpec as P

CH_IN = 640
ADAM_STEP = 10


BETA_ONE = 0.9
BETA_TWO = 0.99
RATE = 0.05
EPSILON = 1e-08


def silu_slope(values):
    sig = jax.nn.sigmoid(values)
    return sig * (1.0 + values * (1.0 - sig))


def forward_taps(activation, kernel_bf):
    side_cells = activation.shape[1]
    cell_count = activation.shape[0] * side_cells * side_cells
    cols_out = kernel_bf.shape[1] // 9
    padded = jnp.pad(activation, ((0, 0), (1, 1), (1, 1), (0, 0)))
    summed = jnp.zeros((cell_count, cols_out), jnp.float32)
    for tap_index in range(9):
        tap_row = tap_index // 3
        tap_col = tap_index % 3
        window = padded[
            :, tap_row : tap_row + side_cells, tap_col : tap_col + side_cells, :
        ].reshape(cell_count, activation.shape[3])
        summed = summed + jnp.dot(
            window,
            kernel_bf[:, tap_index * cols_out : (tap_index + 1) * cols_out],
            preferred_element_type=jnp.float32,
        )
    return summed


def backward_taps(deltas, kernel_bf):
    side_cells = deltas.shape[1]
    cell_count = deltas.shape[0] * side_cells * side_cells
    cols_out = deltas.shape[3]
    padded = jnp.pad(deltas, ((0, 0), (1, 1), (1, 1), (0, 0)))
    summed = jnp.zeros((cell_count, kernel_bf.shape[0]), jnp.float32)
    for tap_index in range(9):
        tap_row = tap_index // 3
        tap_col = tap_index % 3
        window = padded[
            :, 2 - tap_row : 2 - tap_row + side_cells, 2 - tap_col : 2 - tap_col + side_cells, :
        ].reshape(cell_count, cols_out)
        block = kernel_bf[:, tap_index * cols_out : (tap_index + 1) * cols_out]
        summed = summed + lax.dot_general(
            window, block, (((1,), (1,)), ((), ())), preferred_element_type=jnp.float32
        )
    return summed


def weight_taps(activation, deltas):
    side_cells = activation.shape[1]
    cell_count = activation.shape[0] * side_cells * side_cells
    flat_deltas = deltas.reshape(cell_count, deltas.shape[3])
    padded = jnp.pad(activation, ((0, 0), (1, 1), (1, 1), (0, 0)))
    blocks = []
    for tap_index in range(9):
        tap_row = tap_index // 3
        tap_col = tap_index % 3
        window = padded[
            :, tap_row : tap_row + side_cells, tap_col : tap_col + side_cells, :
        ].reshape(cell_count, activation.shape[3])
        blocks.append(
            lax.dot_general(
                window, flat_deltas, (((0,), (0,)), ((), ())), preferred_element_type=jnp.float32
            )
        )
    return jnp.concatenate(blocks, axis=1)


def adam_update(weights_now, first_now, second_now, gradient):
    first_new = BETA_ONE * first_now + (1.0 - BETA_ONE) * gradient
    second_new = BETA_TWO * second_now + (1.0 - BETA_TWO) * gradient * gradient
    first_fix = 1.0 - BETA_ONE**ADAM_STEP
    second_fix = 1.0 - BETA_TWO**ADAM_STEP
    updated = weights_now - RATE * (first_new / first_fix) / (
        jnp.sqrt(second_new / second_fix) + EPSILON
    )
    return (updated, first_new, second_new)


def takers_and_named(sources):
    members = sources.shape[0]
    slots = max(members // 4, 1)
    own = jnp.arange(members, dtype=jnp.int32)
    takers = jnp.argsort(jnp.where(sources == own, 1, 0), stable=True)[:slots]
    return takers, sources[takers]


def carry_over(stacked, takers, named):
    me = lax.axis_index("member")
    sent = [
        jnp.where(named[slot] == me, stacked, jnp.zeros_like(stacked))
        for slot in range(takers.shape[0])
    ]
    arrived = lax.psum(jnp.stack(sent), "member")
    return arrived


def local_plain(latents, cotangent, weights, first_moment, second_moment, sources):
    scale = (9 * CH_IN) ** (-0.5)
    me = lax.axis_index("member")
    takers, named = takers_and_named(sources)
    images = latents[0]
    activation = jax.nn.silu(images.astype(jnp.float32)).astype(jnp.bfloat16)
    kernel_rows = weights[0].astype(jnp.bfloat16)
    state = jnp.concatenate(
        [kernel_rows, first_moment[0].astype(jnp.bfloat16), second_moment[0].astype(jnp.bfloat16)]
    )
    cell_count = images.shape[0] * images.shape[1] * images.shape[2]
    cols_out = cotangent.shape[4]
    kernel_all = lax.all_gather(kernel_rows, "dp", axis=0, tiled=True)
    arrived = carry_over(state, takers, named)
    hidden = scale * forward_taps(activation, kernel_all)
    deltas = (
        cotangent[0].reshape(cell_count, cols_out).astype(jnp.float32) * silu_slope(hidden)
    ).astype(jnp.bfloat16)
    deltas_img = deltas.reshape(cotangent[0].shape)
    back = scale * backward_taps(deltas_img, kernel_all)
    slope_in = silu_slope(images.reshape(cell_count, images.shape[3]).astype(jnp.float32))
    latent_grad = (back * slope_in).astype(jnp.bfloat16).reshape(latents.shape)
    gradient = lax.psum_scatter(
        (scale * weight_taps(activation, deltas_img)).astype(jnp.bfloat16),
        "dp",
        scatter_dimension=0,
        tiled=True,
    )
    gradient, arrived = lax.optimization_barrier((gradient, arrived))
    moved_gradient = carry_over(gradient, takers, named)
    rows = gradient.shape[0]
    weights_now, first_now, second_now = weights[0], first_moment[0], second_moment[0]
    gradient = gradient.astype(jnp.float32)
    for slot in range(takers.shape[0]):
        taking = (takers[slot] == me) & (named[slot] != me)
        moved = arrived[slot].astype(jnp.float32)
        weights_now = jnp.where(taking, moved[:rows], weights_now)
        first_now = jnp.where(taking, moved[rows : 2 * rows], first_now)
        second_now = jnp.where(taking, moved[2 * rows :], second_now)
        gradient = jnp.where(taking, moved_gradient[slot].astype(jnp.float32), gradient)
    updated, first_new, second_new = adam_update(weights_now, first_now, second_now, gradient)
    return (latent_grad, updated[None], first_new[None], second_new[None])


HALF = 48


def shifted(values):
    none = jnp.zeros((1, values.shape[1]), jnp.float32)
    before = jnp.concatenate([none, values[:-1]], axis=0)
    after = jnp.concatenate([values[1:], none], axis=0)
    return before, values, after


def block_kernel(
    sources,
    latents,
    weights,
    cotangent_hbm,
    first_hbm,
    second_hbm,
    latent_grad,
    grad_out,
    weights_out,
    first_out,
    second_out,
    cotangent,
    first_moment,
    second_moment,
    grad,
    kall,
    near,
    act_t,
    total,
    partial,
    core_in,
    chip_sum,
    x_in,
    y_in,
    a_sum,
    b_sum,
    a_in,
    b_in,
    up_in,
    down_in,
    up_grad,
    down_grad,
    ag_send,
    ag_recv,
    rs_send,
    rs_recv,
    z_send,
    z_recv,
    load_sem,
):
    images, side = latents.shape[0], latents.shape[1]
    width = latents.shape[3]
    cells = side * side
    rows = weights.shape[0]
    scale = (9 * CH_IN) ** (-0.5)
    f32, bf16 = jnp.float32, jnp.bfloat16
    k = lax.axis_index("member")
    me = lax.axis_index("dp")
    y, x, c = me // 4, (me // 2) % 2, me % 2
    sib = me + 1 - 2 * c
    xp = me + 2 - 4 * x
    yp = me + 4 - 8 * y
    diag = xp + 4 - 8 * y
    loads = [
        pltpu.make_async_copy(src, dst, load_sem.at[at])
        for at, (src, dst) in enumerate(
            (
                (first_hbm, first_moment),
                (second_hbm, second_moment),
                (cotangent_hbm, cotangent),
            )
        )
    ]
    for load in loads:
        load.start()
    named = jnp.float32(0.0)
    from_below = jnp.float32(0.0)
    taking = jnp.float32(0.0)
    for member in range(4):
        source = sources[member]
        takes = jnp.where(source != member, 1.0, 0.0)
        named += takes * jnp.where(source == k, 1.0, 0.0)
        from_below += takes * jnp.where(source < member, 1.0, 0.0)
        taking += takes * jnp.where(k == member, 1.0, 0.0)

    def remote(src, dst, send, recv, member, index):
        return pltpu.make_async_remote_copy(
            src_ref=src,
            dst_ref=dst,
            send_sem=send,
            recv_sem=recv,
            device_id=(member, index),
            device_id_type=pl.DeviceIdType.MESH,
        )

    barrier = pltpu.get_barrier_semaphore()
    for peer in (sib, xp, yp):
        pl.semaphore_signal(
            barrier, inc=1, device_id=(k, peer), device_id_type=pl.DeviceIdType.MESH
        )

    @pl.when(k < 3)
    def _():
        pl.semaphore_signal(
            barrier, inc=1, device_id=(k + 1, me), device_id_type=pl.DeviceIdType.MESH
        )

    @pl.when(k > 0)
    def _():
        pl.semaphore_signal(
            barrier, inc=1, device_id=(k - 1, me), device_id_type=pl.DeviceIdType.MESH
        )

    pl.semaphore_wait(barrier, 3 + jnp.where(k < 3, 1, 0) + jnp.where(k > 0, 1, 0))

    def block(t, owner, first=0, count=rows):
        return kall.at[t, owner, pl.ds(first, count)]

    def gather(t, kind):
        if kind < 3:
            part, peer = block(t, me), (sib, xp, yp)[kind]
        elif kind == 3:
            part, peer = block(t, xp, 0, HALF), yp
        elif kind == 4:
            part, peer = block(t, yp, HALF, rows - HALF), xp
        else:
            part, peer = block(t, (xp, yp, diag)[kind - 5]), sib
        return remote(part, part, ag_send.at[t, kind], ag_recv.at[t, kind], k, peer)

    def gather_wait(t, kind):
        gather_in(t, kind).wait_recv()

    def gather_in(t, kind):
        if kind < 3:
            part = block(t, (sib, xp, yp)[kind])
        elif kind == 3:
            part = block(t, diag, 0, HALF)
        elif kind == 4:
            part = block(t, diag, HALF, rows - HALF)
        else:
            over = 1 - 2 * c
            part = block(t, (xp + over, yp + over, diag + over)[kind - 5])
        return remote(part, part, ag_send.at[t, kind], ag_recv.at[t, kind], k, sib)

    state = (weights, first_moment, second_moment)

    def columns(t):
        return pl.ds(pl.multiple_of(t * width, 128), width)

    def state_step(tick, lane, rank, here, target):
        j = jnp.where(rank == 0, tick, tick // 2 - 2 * rank)
        even = (tick % 2 == 0) | (rank == 0)

        @pl.when(even & (j >= 0) & (j < 9) & (rank < 3))
        def _():
            @pl.when(rank == 0)
            def _():
                for at in range(3):
                    here[j, at] = state[at][:, columns(j)].astype(bf16)

            @pl.when(rank > 0)
            def _():
                remote(
                    here.at[j], here.at[j], z_send.at[lane, j], z_recv.at[lane, j], target, me
                ).wait_recv()
                for at in range(3):
                    mine, came = state[at][:, columns(j)], here[j, at].astype(f32)
                    here[j, at] = (mine * named + came * (1.0 - named)).astype(bf16)

            remote(
                here.at[j], here.at[j], z_send.at[lane, j], z_recv.at[lane, j], target, me
            ).start()

    def grad_step(tick, lane, rank, here, target):
        t = tick - 14 - 2 * rank

        @pl.when((t >= 0) & (t < 9) & (rank < 3))
        def _():
            copy = remote(
                here.at[t], here.at[t], z_send.at[lane, t], z_recv.at[lane, t], target, me
            )

            @pl.when(rank == 0)
            def _():
                here[t] = grad[t]

            @pl.when(rank > 0)
            def _():
                copy.wait_recv()
                mine, came = grad[t].astype(f32), here[t].astype(f32)
                here[t] = (mine * named + came * (1.0 - named)).astype(bf16)

            copy.start()

    def member_steps(tick, with_grad):
        state_step(tick, 0, k, up_in, jnp.minimum(k + 1, 3))
        state_step(tick, 1, 3 - k, down_in, jnp.maximum(k - 1, 0))
        if with_grad:
            grad_step(tick, 2, k, up_grad, jnp.minimum(k + 1, 3))
            grad_step(tick, 3, 3 - k, down_grad, jnp.maximum(k - 1, 0))

    def cast_tap(t, carry):
        kall[t, me] = weights[:, columns(t)].astype(bf16)
        return carry

    lax.fori_loop(0, 9, cast_tap, 0)

    def first_sends(t):
        for kind in range(3):
            gather(t, kind).start()

    def ahead(t, carry):
        first_sends(t)
        return carry

    lax.fori_loop(0, 4, ahead, 0)

    zero_row = jnp.zeros((side, width), bf16)

    def clear(n, carry):
        near[n // images, n % images, 0] = zero_row
        near[n // images, n % images, side + 1] = zero_row
        return carry

    lax.fori_loop(0, 3 * images, clear, 0)

    def activate(n, carry):
        b, i = n // side, n % side
        value = latents[b, i].astype(f32)
        value = value / (1.0 + jnp.exp(-value))
        for at, moved_values in enumerate(shifted(value)):
            near[at, b, i + 1] = moved_values.astype(bf16)
        return carry

    def turn(b):
        flat = near[1, b, 1 : side + 1].reshape(cells, width)
        act_t[b] = jnp.transpose(flat)

    for load in loads:
        load.wait()

    def forward(i, carry):
        @pl.when(i < 9)
        def _():
            member_steps(i, False)

        @pl.when(i + 4 < 9)
        def _():
            first_sends(i + 4)

        @pl.when(i < 9)
        def _():
            gather_wait(i, 1)
            gather_wait(i, 2)
            for kind in (3, 4, 5, 6):
                gather(i, kind).start()

        @pl.when((i >= 1) & (i < 10))
        def _():
            gather_wait(i - 1, 3)
            gather_wait(i - 1, 4)
            gather(i - 1, 7).start()

        half_rows = images * side // 2

        @pl.when(i < 2)
        def _():
            lax.fori_loop(i * half_rows, (i + 1) * half_rows, activate, 0)

        @pl.when((i >= 2) & (i < 2 + images))
        def _():
            turn(i - 2)

        @pl.when(i >= 2)
        def _():
            t = i - 2
            for kind in (0, 5, 6, 7):
                gather_wait(t, kind)
            weight = kall[t].reshape(8 * rows, width)

            window = near[t % 3, :, pl.ds(t // 3, side)].reshape(images * cells, width)
            product = jnp.dot(window, weight, preferred_element_type=f32)

            @pl.when(t == 0)
            def _():
                total[...] = product

            @pl.when(t > 0)
            def _():
                total[...] += product

        return carry

    lax.fori_loop(0, 11, forward, 0)

    def slope_rows(n, carry):
        b, i = n // side, n % side
        hidden = scale * total[pl.ds(pl.multiple_of(n * side, side), side)]
        value = cotangent[b, i].astype(f32) * silu_slope(hidden)
        for at, moved_values in enumerate(shifted(value)):
            near[at, b, i + 1] = moved_values.astype(bf16)
        return carry

    lax.fori_loop(0, images * side, slope_rows, 0, unroll=4)

    def scatter(t, kind):
        if kind == 0:
            src, dst, peer = partial.at[t, :, :, 1 - c], core_in.at[t], sib
        elif kind == 1:
            src, dst, peer = chip_sum.at[t, :, 1 - x, pl.ds(0, HALF)], x_in.at[t], xp
        elif kind == 2:
            src, dst, peer = chip_sum.at[t, 1 - y, :, pl.ds(HALF, rows - HALF)], y_in.at[t], yp
        elif kind == 3:
            src, dst, peer = a_sum.at[t, 1 - y], a_in.at[t], yp
        else:
            src, dst, peer = b_sum.at[t, 1 - x], b_in.at[t], xp
        return remote(src, dst, rs_send.at[t, kind], rs_recv.at[t, kind], k, peer)

    def plus(one, two):
        return (one.astype(f32) + two.astype(f32)).astype(bf16)

    def scatter_steps(i):
        @pl.when((i >= 1) & (i < 10))
        def _():
            t = i - 1
            scatter(t, 0).wait_recv()
            for yy in range(2):
                for xx in range(2):
                    chip_sum[t, yy, xx] = plus(partial[t, yy, xx, c], core_in[t, yy, xx])
            scatter(t, 1).start()
            scatter(t, 2).start()

        @pl.when((i >= 3) & (i < 12))
        def _():
            t = i - 3
            scatter(t, 1).wait_recv()
            scatter(t, 2).wait_recv()
            for at in range(2):
                a_sum[t, at] = plus(chip_sum[t, at, x, 0:HALF], x_in[t, at])
                b_sum[t, at] = plus(chip_sum[t, y, at, HALF:rows], y_in[t, at])
            scatter(t, 3).start()
            scatter(t, 4).start()

        @pl.when((i >= 5) & (i < 14))
        def _():
            t = i - 5
            scatter(t, 3).wait_recv()
            scatter(t, 4).wait_recv()
            grad[t, 0:HALF] = plus(a_sum[t, y], a_in[t])
            grad[t, HALF:rows] = plus(b_sum[t, x], b_in[t])

    def kernel_grad(t, carry):
        scatter_steps(t)
        member_steps(t + 9, True)
        window = near[2 - t % 3, :, pl.ds(2 - t // 3, side)].reshape(images * cells, width)

        lhs = jnp.concatenate([act_t[b] for b in range(images)], axis=1)
        product = scale * jnp.dot(lhs, window, preferred_element_type=f32)
        partial[t] = product.astype(bf16).reshape(2, 2, 2, rows, width)
        scatter(t, 0).start()
        return carry

    lax.fori_loop(0, 9, kernel_grad, 0)

    def back(r, carry):
        def tick(col):
            scatter_steps(3 * r + col + 9)
            member_steps(3 * r + col + 18, True)

        weight = jnp.concatenate(
            [kall[3 * r + col].reshape(8 * rows, width) for col in range(3)], axis=1
        )
        pair = images // 2
        for part in range(2):
            windows = jnp.concatenate(
                [
                    near[2 - col, part * pair : (part + 1) * pair, pl.ds(2 - r, side)].reshape(
                        pair * cells, width
                    )
                    for col in range(3)
                ],
                axis=1,
            )
            product = lax.dot_general(
                windows, weight, (((1,), (1,)), ((), ())), preferred_element_type=f32
            )
            here = pl.ds(part * pair * cells, pair * cells)

            @pl.when(r == 0)
            def _():
                total[here] = product

            @pl.when(r > 0)
            def _():
                total[here] += product

            tick(part)
        tick(2)
        return carry

    lax.fori_loop(0, 3, back, 0)

    def finish(n, carry):
        b, i = n // side, n % side
        value = scale * total[pl.ds(pl.multiple_of(n * side, side), side)]
        value = value * silu_slope(latents[b, i].astype(f32))
        latent_grad[b, i] = value.astype(bf16)
        return carry

    lax.fori_loop(0, images * side, finish, 0, unroll=4)

    def mix(lower, upper, share):
        return (lower.astype(f32) * share + upper.astype(f32) * (1.0 - share)).astype(bf16)

    def pick(j):
        def store(below, above, share):
            for at, out in enumerate((weights_out, first_out, second_out)):
                out[:, columns(j)] = mix(below[0][j, at], above[0][j, at], share)
            came = mix(below[1][j], above[1][j], share)
            grad_out[:, columns(j)] = mix(came, grad[j], taking)

        low, high = (up_in, up_grad), (down_in, down_grad)

        @pl.when(k == 0)
        def _():
            store(high, high, 1.0)

        @pl.when(k == 3)
        def _():
            store(low, low, 1.0)

        @pl.when((k > 0) & (k < 3))
        def _():
            store(low, high, from_below)

    def drain(j, carry):
        for lane, here in enumerate((up_in, down_in, up_grad, down_grad)):
            copy = remote(here.at[j], here.at[j], z_send.at[lane, j], z_recv.at[lane, j], k, sib)
            last = k == 3 if lane % 2 == 0 else k == 0

            @pl.when(last)
            def _():
                copy.wait_recv()

            @pl.when(jnp.logical_not(last))
            def _():
                copy.wait_send()

        pick(j)
        for kind in range(8):
            gather(j, kind).wait_send()
        for kind in range(5):
            scatter(j, kind).wait_send()
        return carry

    lax.fori_loop(0, 9, drain, 0)


def local_block(latents, cotangent, weights, first_moment, second_moment, sources):
    me = lax.axis_index("member")
    members = jnp.arange(4, dtype=jnp.int32)
    taking = jnp.any((sources != members) & (members == me))
    rows, width = weights.shape[1], latents.shape[4]
    bf16 = jnp.bfloat16
    flat = (rows, 9 * width)
    images, side = latents.shape[1], latents.shape[2]
    cells = side * side
    vmem = pl.BlockSpec(memory_space=pltpu.VMEM)
    tap = (9, rows, width)
    half, rest = HALF, rows - HALF
    latent_grad, grad, weights_in, first_in, second_in = pl.pallas_call(
        block_kernel,
        out_shape=(
            jax.ShapeDtypeStruct(latents.shape[1:], bf16),
        )
        + (jax.ShapeDtypeStruct(flat, bf16),) * 4,
        in_specs=[pl.BlockSpec(memory_space=pltpu.SMEM), vmem, vmem]
        + [pl.BlockSpec(memory_space=pl.ANY)] * 3,
        out_specs=(vmem,) * 5,
        scratch_shapes=[
            pltpu.VMEM(latents.shape[1:], bf16),
            pltpu.VMEM(flat, jnp.float32),
            pltpu.VMEM(flat, jnp.float32),
            pltpu.VMEM(tap, bf16),
            pltpu.VMEM((9, 8, rows, width), bf16),
            pltpu.VMEM((3, images, side + 2, side, width), bf16),
            pltpu.VMEM((images, width, cells), bf16),
            pltpu.VMEM((images * cells, width), jnp.float32),
            pltpu.VMEM((9, 2, 2, 2, rows, width), bf16),
            pltpu.VMEM((9, 2, 2, rows, width), bf16),
            pltpu.VMEM((9, 2, 2, rows, width), bf16),
            pltpu.VMEM((9, 2, half, width), bf16),
            pltpu.VMEM((9, 2, rest, width), bf16),
            pltpu.VMEM((9, 2, half, width), bf16),
            pltpu.VMEM((9, 2, rest, width), bf16),
            pltpu.VMEM((9, half, width), bf16),
            pltpu.VMEM((9, rest, width), bf16),
            pltpu.VMEM((9, 3, rows, width), bf16),
            pltpu.VMEM((9, 3, rows, width), bf16),
            pltpu.VMEM(tap, bf16),
            pltpu.VMEM(tap, bf16),
            pltpu.SemaphoreType.DMA((9, 8)),
            pltpu.SemaphoreType.DMA((9, 8)),
            pltpu.SemaphoreType.DMA((9, 5)),
            pltpu.SemaphoreType.DMA((9, 5)),
            pltpu.SemaphoreType.DMA((4, 9)),
            pltpu.SemaphoreType.DMA((4, 9)),
            pltpu.SemaphoreType.DMA((3,)),
        ],
        compiler_params=pltpu.CompilerParams(
            collective_id=0, has_side_effects=True, vmem_limit_bytes=60 * 1024 * 1024
        ),
        cost_estimate=pl.CostEstimate(
            flops=6 * images * cells * 9 * width * width, bytes_accessed=16000000, transcendentals=0
        ),
    )(sources, latents[0], weights[0], cotangent[0], first_moment[0], second_moment[0])

    f32 = jnp.float32
    weights_now = jnp.where(taking, weights_in.astype(f32), weights[0])
    first_now = jnp.where(taking, first_in.astype(f32), first_moment[0])
    second_now = jnp.where(taking, second_in.astype(f32), second_moment[0])
    gradient = grad.astype(f32)
    updated, first_new, second_new = adam_update(weights_now, first_now, second_now, gradient)
    return (latent_grad[None], updated[None], first_new[None], second_new[None])


def solution(mesh):
    fits = mesh.shape["member"] == 4 and mesh.shape["dp"] == 8
    local = local_block if fits else local_plain
    in_specs = (
        P("member", "dp", None, None, None),
        P("member", "dp", None, None, None),
        P("member", "dp", None),
        P("member", "dp", None),
        P("member", "dp", None),
        P(),
    )
    out_specs = (
        P("member", "dp", None, None, None),
        P("member", "dp", None),
        P("member", "dp", None),
        P("member", "dp", None),
    )
    return jax.shard_map(local, mesh=mesh, in_specs=in_specs, out_specs=out_specs, check_vma=False)
```

```python
import jax
import jax.numpy as jnp
from jax import lax
from jax.experimental import pallas as pl
from jax.experimental.pallas import tpu as pltpu
from jax.sharding import PartitionSpec as P

CH_IN = 640
ADAM_STEP = 10


BETA_ONE = 0.9
BETA_TWO = 0.99
RATE = 0.05
EPSILON = 1e-08


def silu_slope(values):
    sig = jax.nn.sigmoid(values)
    return sig * (1.0 + values * (1.0 - sig))


def forward_taps(activation, kernel_bf):
    side_cells = activation.shape[1]
    cell_count = activation.shape[0] * side_cells * side_cells
    cols_out = kernel_bf.shape[1] // 9
    padded = jnp.pad(activation, ((0, 0), (1, 1), (1, 1), (0, 0)))
    summed = jnp.zeros((cell_count, cols_out), jnp.float32)
    for tap_index in range(9):
        tap_row = tap_index // 3
        tap_col = tap_index % 3
        window = padded[
            :, tap_row : tap_row + side_cells, tap_col : tap_col + side_cells, :
        ].reshape(cell_count, activation.shape[3])
        summed = summed + jnp.dot(
            window,
            kernel_bf[:, tap_index * cols_out : (tap_index + 1) * cols_out],
            preferred_element_type=jnp.float32,
        )
    return summed


def backward_taps(deltas, kernel_bf):
    side_cells = deltas.shape[1]
    cell_count = deltas.shape[0] * side_cells * side_cells
    cols_out = deltas.shape[3]
    padded = jnp.pad(deltas, ((0, 0), (1, 1), (1, 1), (0, 0)))
    summed = jnp.zeros((cell_count, kernel_bf.shape[0]), jnp.float32)
    for tap_index in range(9):
        tap_row = tap_index // 3
        tap_col = tap_index % 3
        window = padded[
            :, 2 - tap_row : 2 - tap_row + side_cells, 2 - tap_col : 2 - tap_col + side_cells, :
        ].reshape(cell_count, cols_out)
        block = kernel_bf[:, tap_index * cols_out : (tap_index + 1) * cols_out]
        summed = summed + lax.dot_general(
            window, block, (((1,), (1,)), ((), ())), preferred_element_type=jnp.float32
        )
    return summed


def weight_taps(activation, deltas):
    side_cells = activation.shape[1]
    cell_count = activation.shape[0] * side_cells * side_cells
    flat_deltas = deltas.reshape(cell_count, deltas.shape[3])
    padded = jnp.pad(activation, ((0, 0), (1, 1), (1, 1), (0, 0)))
    blocks = []
    for tap_index in range(9):
        tap_row = tap_index // 3
        tap_col = tap_index % 3
        window = padded[
            :, tap_row : tap_row + side_cells, tap_col : tap_col + side_cells, :
        ].reshape(cell_count, activation.shape[3])
        blocks.append(
            lax.dot_general(
                window, flat_deltas, (((0,), (0,)), ((), ())), preferred_element_type=jnp.float32
            )
        )
    return jnp.concatenate(blocks, axis=1)


def adam_update(weights_now, first_now, second_now, gradient):
    first_new = BETA_ONE * first_now + (1.0 - BETA_ONE) * gradient
    second_new = BETA_TWO * second_now + (1.0 - BETA_TWO) * gradient * gradient
    first_fix = 1.0 - BETA_ONE**ADAM_STEP
    second_fix = 1.0 - BETA_TWO**ADAM_STEP
    updated = weights_now - RATE * (first_new / first_fix) / (
        jnp.sqrt(second_new / second_fix) + EPSILON
    )
    return (updated, first_new, second_new)


def takers_and_named(sources):
    members = sources.shape[0]
    slots = max(members // 4, 1)
    own = jnp.arange(members, dtype=jnp.int32)
    takers = jnp.argsort(jnp.where(sources == own, 1, 0), stable=True)[:slots]
    return takers, sources[takers]


def carry_over(stacked, takers, named):
    me = lax.axis_index("member")
    sent = [
        jnp.where(named[slot] == me, stacked, jnp.zeros_like(stacked))
        for slot in range(takers.shape[0])
    ]
    arrived = lax.psum(jnp.stack(sent), "member")
    return arrived


def local_plain(latents, cotangent, weights, first_moment, second_moment, sources):
    scale = (9 * CH_IN) ** (-0.5)
    me = lax.axis_index("member")
    takers, named = takers_and_named(sources)
    images = latents[0]
    activation = jax.nn.silu(images.astype(jnp.float32)).astype(jnp.bfloat16)
    kernel_rows = weights[0].astype(jnp.bfloat16)
    state = jnp.concatenate(
        [kernel_rows, first_moment[0].astype(jnp.bfloat16), second_moment[0].astype(jnp.bfloat16)]
    )
    cell_count = images.shape[0] * images.shape[1] * images.shape[2]
    cols_out = cotangent.shape[4]
    kernel_all = lax.all_gather(kernel_rows, "dp", axis=0, tiled=True)
    arrived = carry_over(state, takers, named)
    hidden = scale * forward_taps(activation, kernel_all)
    deltas = (
        cotangent[0].reshape(cell_count, cols_out).astype(jnp.float32) * silu_slope(hidden)
    ).astype(jnp.bfloat16)
    deltas_img = deltas.reshape(cotangent[0].shape)
    back = scale * backward_taps(deltas_img, kernel_all)
    slope_in = silu_slope(images.reshape(cell_count, images.shape[3]).astype(jnp.float32))
    latent_grad = (back * slope_in).astype(jnp.bfloat16).reshape(latents.shape)
    gradient = lax.psum_scatter(
        (scale * weight_taps(activation, deltas_img)).astype(jnp.bfloat16),
        "dp",
        scatter_dimension=0,
        tiled=True,
    )
    gradient, arrived = lax.optimization_barrier((gradient, arrived))
    moved_gradient = carry_over(gradient, takers, named)
    rows = gradient.shape[0]
    weights_now, first_now, second_now = weights[0], first_moment[0], second_moment[0]
    gradient = gradient.astype(jnp.float32)
    for slot in range(takers.shape[0]):
        taking = (takers[slot] == me) & (named[slot] != me)
        moved = arrived[slot].astype(jnp.float32)
        weights_now = jnp.where(taking, moved[:rows], weights_now)
        first_now = jnp.where(taking, moved[rows : 2 * rows], first_now)
        second_now = jnp.where(taking, moved[2 * rows :], second_now)
        gradient = jnp.where(taking, moved_gradient[slot].astype(jnp.float32), gradient)
    updated, first_new, second_new = adam_update(weights_now, first_now, second_now, gradient)
    return (latent_grad, updated[None], first_new[None], second_new[None])


HALF = 48


def shifted(values):
    none = jnp.zeros((1, values.shape[1]), jnp.float32)
    before = jnp.concatenate([none, values[:-1]], axis=0)
    after = jnp.concatenate([values[1:], none], axis=0)
    return before, values, after


def block_kernel(
    sources,
    latents,
    weights,
    cotangent_hbm,
    first_hbm,
    second_hbm,
    latent_grad,
    grad_out,
    weights_out,
    first_out,
    second_out,
    cotangent,
    first_moment,
    second_moment,
    grad,
    kall,
    near,
    act_t,
    total,
    partial,
    core_in,
    chip_sum,
    x_in,
    y_in,
    a_sum,
    b_sum,
    a_in,
    b_in,
    up_in,
    down_in,
    up_grad,
    down_grad,
    ag_send,
    ag_recv,
    rs_send,
    rs_recv,
    z_send,
    z_recv,
    load_sem,
):
    images, side = latents.shape[0], latents.shape[1]
    width = latents.shape[3]
    cells = side * side
    rows = weights.shape[0]
    scale = (9 * CH_IN) ** (-0.5)
    f32, bf16 = jnp.float32, jnp.bfloat16
    k = lax.axis_index("member")
    me = lax.axis_index("dp")
    y, x, c = me // 4, (me // 2) % 2, me % 2
    sib = me + 1 - 2 * c
    xp = me + 2 - 4 * x
    yp = me + 4 - 8 * y
    diag = xp + 4 - 8 * y
    loads = [
        pltpu.make_async_copy(src, dst, load_sem.at[at])
        for at, (src, dst) in enumerate(
            (
                (first_hbm, first_moment),
                (second_hbm, second_moment),
                (cotangent_hbm, cotangent),
            )
        )
    ]
    for load in loads:
        load.start()
    named = jnp.float32(0.0)
    from_below = jnp.float32(0.0)
    taking = jnp.float32(0.0)
    for member in range(4):
        source = sources[member]
        takes = jnp.where(source != member, 1.0, 0.0)
        named += takes * jnp.where(source == k, 1.0, 0.0)
        from_below += takes * jnp.where(source < member, 1.0, 0.0)
        taking += takes * jnp.where(k == member, 1.0, 0.0)

    def remote(src, dst, send, recv, member, index):
        return pltpu.make_async_remote_copy(
            src_ref=src,
            dst_ref=dst,
            send_sem=send,
            recv_sem=recv,
            device_id=(member, index),
            device_id_type=pl.DeviceIdType.MESH,
        )

    barrier = pltpu.get_barrier_semaphore()
    for peer in (sib, xp, yp):
        pl.semaphore_signal(
            barrier, inc=1, device_id=(k, peer), device_id_type=pl.DeviceIdType.MESH
        )

    @pl.when(k < 3)
    def _():
        pl.semaphore_signal(
            barrier, inc=1, device_id=(k + 1, me), device_id_type=pl.DeviceIdType.MESH
        )

    @pl.when(k > 0)
    def _():
        pl.semaphore_signal(
            barrier, inc=1, device_id=(k - 1, me), device_id_type=pl.DeviceIdType.MESH
        )

    pl.semaphore_wait(barrier, 3 + jnp.where(k < 3, 1, 0) + jnp.where(k > 0, 1, 0))

    def block(t, owner, first=0, count=rows):
        return kall.at[t, owner, pl.ds(first, count)]

    def gather(t, kind):
        if kind < 3:
            part, peer = block(t, me), (sib, xp, yp)[kind]
        elif kind == 3:
            part, peer = block(t, xp, 0, HALF), yp
        elif kind == 4:
            part, peer = block(t, yp, HALF, rows - HALF), xp
        else:
            part, peer = block(t, (xp, yp, diag)[kind - 5]), sib
        return remote(part, part, ag_send.at[t, kind], ag_recv.at[t, kind], k, peer)

    def gather_wait(t, kind):
        gather_in(t, kind).wait_recv()

    def gather_in(t, kind):
        if kind < 3:
            part = block(t, (sib, xp, yp)[kind])
        elif kind == 3:
            part = block(t, diag, 0, HALF)
        elif kind == 4:
            part = block(t, diag, HALF, rows - HALF)
        else:
            over = 1 - 2 * c
            part = block(t, (xp + over, yp + over, diag + over)[kind - 5])
        return remote(part, part, ag_send.at[t, kind], ag_recv.at[t, kind], k, sib)

    state = (weights, first_moment, second_moment)

    def columns(t):
        return pl.ds(pl.multiple_of(t * width, 128), width)

    def state_step(tick, lane, rank, here, target):
        j = jnp.where(rank == 0, tick, (tick - 1) // 2 - rank)
        due = (tick % 2 == 1) | (rank == 0)

        @pl.when(due & (j >= 0) & (j < 9) & (rank < 3))
        def _():
            @pl.when(rank == 0)
            def _():
                for at in range(3):
                    here[j, at] = state[at][:, columns(j)].astype(bf16)

            @pl.when(rank > 0)
            def _():
                remote(
                    here.at[j], here.at[j], z_send.at[lane, j], z_recv.at[lane, j], target, me
                ).wait_recv()
                for at in range(3):
                    mine, came = state[at][:, columns(j)], here[j, at].astype(f32)
                    here[j, at] = (mine * named + came * (1.0 - named)).astype(bf16)

            remote(
                here.at[j], here.at[j], z_send.at[lane, j], z_recv.at[lane, j], target, me
            ).start()

    def grad_step(tick, lane, rank, here, target):
        t = tick - 16 - 2 * rank

        @pl.when((t >= 0) & (t < 9) & (rank < 3))
        def _():
            copy = remote(
                here.at[t], here.at[t], z_send.at[lane, t], z_recv.at[lane, t], target, me
            )

            @pl.when(rank == 0)
            def _():
                here[t] = grad[t]

            @pl.when(rank > 0)
            def _():
                copy.wait_recv()
                mine, came = grad[t].astype(f32), here[t].astype(f32)
                here[t] = (mine * named + came * (1.0 - named)).astype(bf16)

            copy.start()

    def member_steps(tick, with_grad):
        state_step(tick, 0, k, up_in, jnp.minimum(k + 1, 3))
        state_step(tick, 1, 3 - k, down_in, jnp.maximum(k - 1, 0))
        if with_grad:
            grad_step(tick, 2, k, up_grad, jnp.minimum(k + 1, 3))
            grad_step(tick, 3, 3 - k, down_grad, jnp.maximum(k - 1, 0))

    def cast_tap(t, carry):
        kall[t, me] = weights[:, columns(t)].astype(bf16)
        return carry

    lax.fori_loop(0, 9, cast_tap, 0)

    def first_sends(t):
        for kind in range(3):
            gather(t, kind).start()

    def ahead(t, carry):
        first_sends(t)
        return carry

    lax.fori_loop(0, 4, ahead, 0)

    zero_row = jnp.zeros((side, width), bf16)

    def clear(n, carry):
        near[n // images, n % images, 0] = zero_row
        near[n // images, n % images, side + 1] = zero_row
        return carry

    lax.fori_loop(0, 3 * images, clear, 0)

    def activate(n, carry):
        b, i = n // side, n % side
        value = latents[b, i].astype(f32)
        value = value / (1.0 + jnp.exp(-value))
        for at, moved_values in enumerate(shifted(value)):
            near[at, b, i + 1] = moved_values.astype(bf16)
        return carry

    def turn(b):
        flat = near[1, b, 1 : side + 1].reshape(cells, width)
        act_t[b] = jnp.transpose(flat)

    for load in loads:
        load.wait()

    def forward(i, carry):
        member_steps(i, False)

        @pl.when(i + 4 < 9)
        def _():
            first_sends(i + 4)

        @pl.when(i < 9)
        def _():
            gather_wait(i, 1)
            gather_wait(i, 2)
            for kind in (3, 4, 5, 6):
                gather(i, kind).start()

        @pl.when((i >= 1) & (i < 10))
        def _():
            gather_wait(i - 1, 3)
            gather_wait(i - 1, 4)
            gather(i - 1, 7).start()

        half_rows = images * side // 2

        @pl.when(i < 2)
        def _():
            lax.fori_loop(0, half_rows, lambda n, carry: activate(n + i * half_rows, carry), 0, unroll=4)

        @pl.when((i >= 2) & (i < 2 + images))
        def _():
            turn(i - 2)

        @pl.when(i >= 2)
        def _():
            t = i - 2
            for kind in (0, 5, 6, 7):
                gather_wait(t, kind)
            weight = kall[t].reshape(8 * rows, width)

            window = near[t % 3, :, pl.ds(t // 3, side)].reshape(images * cells, width)
            product = jnp.dot(window, weight, preferred_element_type=f32)

            @pl.when(t == 0)
            def _():
                total[...] = product

            @pl.when(t > 0)
            def _():
                total[...] += product

        return carry

    lax.fori_loop(0, 11, forward, 0)

    def slope_rows(n, carry):
        b, i = n // side, n % side
        hidden = scale * total[pl.ds(pl.multiple_of(n * side, side), side)]
        value = cotangent[b, i].astype(f32) * silu_slope(hidden)
        for at, moved_values in enumerate(shifted(value)):
            near[at, b, i + 1] = moved_values.astype(bf16)
        return carry

    lax.fori_loop(0, images * side, slope_rows, 0, unroll=4)

    def scatter(t, kind):
        if kind == 0:
            src, dst, peer = partial.at[t, :, :, 1 - c], core_in.at[t], sib
        elif kind == 1:
            src, dst, peer = chip_sum.at[t, :, 1 - x, pl.ds(0, HALF)], x_in.at[t], xp
        elif kind == 2:
            src, dst, peer = chip_sum.at[t, 1 - y, :, pl.ds(HALF, rows - HALF)], y_in.at[t], yp
        elif kind == 3:
            src, dst, peer = a_sum.at[t, 1 - y], a_in.at[t], yp
        else:
            src, dst, peer = b_sum.at[t, 1 - x], b_in.at[t], xp
        return remote(src, dst, rs_send.at[t, kind], rs_recv.at[t, kind], k, peer)

    def plus(one, two):
        return (one.astype(f32) + two.astype(f32)).astype(bf16)

    def scatter_steps(i):
        @pl.when((i >= 1) & (i < 10))
        def _():
            t = i - 1
            scatter(t, 0).wait_recv()
            for yy in range(2):
                for xx in range(2):
                    chip_sum[t, yy, xx] = plus(partial[t, yy, xx, c], core_in[t, yy, xx])
            scatter(t, 1).start()
            scatter(t, 2).start()

        @pl.when((i >= 3) & (i < 12))
        def _():
            t = i - 3
            scatter(t, 1).wait_recv()
            scatter(t, 2).wait_recv()
            for at in range(2):
                a_sum[t, at] = plus(chip_sum[t, at, x, 0:HALF], x_in[t, at])
                b_sum[t, at] = plus(chip_sum[t, y, at, HALF:rows], y_in[t, at])
            scatter(t, 3).start()
            scatter(t, 4).start()

        @pl.when((i >= 5) & (i < 14))
        def _():
            t = i - 5
            scatter(t, 3).wait_recv()
            scatter(t, 4).wait_recv()
            grad[t, 0:HALF] = plus(a_sum[t, y], a_in[t])
            grad[t, HALF:rows] = plus(b_sum[t, x], b_in[t])

    def kernel_grad(t, carry):
        scatter_steps(t)
        member_steps(t + 11, True)
        window = near[2 - t % 3, :, pl.ds(2 - t // 3, side)].reshape(images * cells, width)

        lhs = jnp.concatenate([act_t[b] for b in range(images)], axis=1)
        product = scale * jnp.dot(lhs, window, preferred_element_type=f32)
        partial[t] = product.astype(bf16).reshape(2, 2, 2, rows, width)
        scatter(t, 0).start()
        return carry

    lax.fori_loop(0, 9, kernel_grad, 0)

    def back(r, carry):
        def tick(col):
            scatter_steps(3 * r + col + 9)
            member_steps(3 * r + col + 20, True)

        weight = jnp.concatenate(
            [kall[3 * r + col].reshape(8 * rows, width) for col in range(3)], axis=1
        )
        pair = images // 2
        for part in range(2):
            windows = jnp.concatenate(
                [
                    near[2 - col, part * pair : (part + 1) * pair, pl.ds(2 - r, side)].reshape(
                        pair * cells, width
                    )
                    for col in range(3)
                ],
                axis=1,
            )
            product = lax.dot_general(
                windows, weight, (((1,), (1,)), ((), ())), preferred_element_type=f32
            )
            here = pl.ds(part * pair * cells, pair * cells)

            @pl.when(r == 0)
            def _():
                total[here] = product

            @pl.when(r > 0)
            def _():
                total[here] += product

            tick(part)
        tick(2)
        return carry

    lax.fori_loop(0, 3, back, 0)

    def finish(n, carry):
        b, i = n // side, n % side
        value = scale * total[pl.ds(pl.multiple_of(n * side, side), side)]
        value = value * silu_slope(latents[b, i].astype(f32))
        latent_grad[b, i] = value.astype(bf16)
        return carry

    def mix(lower, upper, share):
        return (lower.astype(f32) * share + upper.astype(f32) * (1.0 - share)).astype(bf16)

    low, high = (up_in, up_grad), (down_in, down_grad)

    def by_place(store):
        @pl.when(k == 0)
        def _():
            store(high, high, 1.0)

        @pl.when(k == 3)
        def _():
            store(low, low, 1.0)

        @pl.when((k > 0) & (k < 3))
        def _():
            store(low, high, from_below)

    def settle(lanes, j):
        for lane, here in lanes:
            copy = remote(here.at[j], here.at[j], z_send.at[lane, j], z_recv.at[lane, j], k, sib)
            last = k == 3 if lane % 2 == 0 else k == 0

            @pl.when(last)
            def _():
                copy.wait_recv()

            @pl.when(jnp.logical_not(last))
            def _():
                copy.wait_send()

    def drain_state(j, carry):
        settle(((0, up_in), (1, down_in)), j)

        def store(below, above, share):
            for at, out in enumerate((weights_out, first_out, second_out)):
                out[:, columns(j)] = mix(below[0][j, at], above[0][j, at], share)

        by_place(store)
        for kind in range(8):
            gather(j, kind).wait_send()
        for kind in range(5):
            scatter(j, kind).wait_send()
        return carry

    def drain_grad(j, carry):
        settle(((2, up_grad), (3, down_grad)), j)

        def store(below, above, share):
            came = mix(below[1][j], above[1][j], share)
            grad_out[:, columns(j)] = mix(came, grad[j], taking)

        by_place(store)
        return carry

    lax.fori_loop(0, 9, drain_state, 0)
    lax.fori_loop(0, images * side, finish, 0, unroll=4)
    lax.fori_loop(0, 9, drain_grad, 0)


def local_block(latents, cotangent, weights, first_moment, second_moment, sources):
    me = lax.axis_index("member")
    members = jnp.arange(4, dtype=jnp.int32)
    taking = jnp.any((sources != members) & (members == me))
    rows, width = weights.shape[1], latents.shape[4]
    bf16 = jnp.bfloat16
    flat = (rows, 9 * width)
    images, side = latents.shape[1], latents.shape[2]
    cells = side * side
    vmem = pl.BlockSpec(memory_space=pltpu.VMEM)
    tap = (9, rows, width)
    half, rest = HALF, rows - HALF
    latent_grad, grad, weights_in, first_in, second_in = pl.pallas_call(
        block_kernel,
        out_shape=(
            jax.ShapeDtypeStruct(latents.shape[1:], bf16),
        )
        + (jax.ShapeDtypeStruct(flat, bf16),) * 4,
        in_specs=[pl.BlockSpec(memory_space=pltpu.SMEM), vmem, vmem]
        + [pl.BlockSpec(memory_space=pl.ANY)] * 3,
        out_specs=(vmem,) * 5,
        scratch_shapes=[
            pltpu.VMEM(latents.shape[1:], bf16),
            pltpu.VMEM(flat, jnp.float32),
            pltpu.VMEM(flat, jnp.float32),
            pltpu.VMEM(tap, bf16),
            pltpu.VMEM((9, 8, rows, width), bf16),
            pltpu.VMEM((3, images, side + 2, side, width), bf16),
            pltpu.VMEM((images, width, cells), bf16),
            pltpu.VMEM((images * cells, width), jnp.float32),
            pltpu.VMEM((9, 2, 2, 2, rows, width), bf16),
            pltpu.VMEM((9, 2, 2, rows, width), bf16),
            pltpu.VMEM((9, 2, 2, rows, width), bf16),
            pltpu.VMEM((9, 2, half, width), bf16),
            pltpu.VMEM((9, 2, rest, width), bf16),
            pltpu.VMEM((9, 2, half, width), bf16),
            pltpu.VMEM((9, 2, rest, width), bf16),
            pltpu.VMEM((9, half, width), bf16),
            pltpu.VMEM((9, rest, width), bf16),
            pltpu.VMEM((9, 3, rows, width), bf16),
            pltpu.VMEM((9, 3, rows, width), bf16),
            pltpu.VMEM(tap, bf16),
            pltpu.VMEM(tap, bf16),
            pltpu.SemaphoreType.DMA((9, 8)),
            pltpu.SemaphoreType.DMA((9, 8)),
            pltpu.SemaphoreType.DMA((9, 5)),
            pltpu.SemaphoreType.DMA((9, 5)),
            pltpu.SemaphoreType.DMA((4, 9)),
            pltpu.SemaphoreType.DMA((4, 9)),
            pltpu.SemaphoreType.DMA((3,)),
        ],
        compiler_params=pltpu.CompilerParams(
            collective_id=0, has_side_effects=True, vmem_limit_bytes=60 * 1024 * 1024
        ),
        cost_estimate=pl.CostEstimate(
            flops=6 * images * cells * 9 * width * width, bytes_accessed=16000000, transcendentals=0
        ),
    )(sources, latents[0], weights[0], cotangent[0], first_moment[0], second_moment[0])

    f32 = jnp.float32
    weights_now = jnp.where(taking, weights_in.astype(f32), weights[0])
    first_now = jnp.where(taking, first_in.astype(f32), first_moment[0])
    second_now = jnp.where(taking, second_in.astype(f32), second_moment[0])
    gradient = grad.astype(f32)
    updated, first_new, second_new = adam_update(weights_now, first_now, second_now, gradient)
    return (latent_grad[None], updated[None], first_new[None], second_new[None])


def solution(mesh):
    fits = mesh.shape["member"] == 4 and mesh.shape["dp"] == 8
    local = local_block if fits else local_plain
    in_specs = (
        P("member", "dp", None, None, None),
        P("member", "dp", None, None, None),
        P("member", "dp", None),
        P("member", "dp", None),
        P("member", "dp", None),
        P(),
    )
    out_specs = (
        P("member", "dp", None, None, None),
        P("member", "dp", None),
        P("member", "dp", None),
        P("member", "dp", None),
    )
    return jax.shard_map(local, mesh=mesh, in_specs=in_specs, out_specs=out_specs, check_vma=False)
```

```python
import jax
import jax.numpy as jnp
from jax import lax
from jax.experimental import pallas as pl
from jax.experimental.pallas import tpu as pltpu
from jax.sharding import PartitionSpec as P

CH_IN = 640
ADAM_STEP = 10


BETA_ONE = 0.9
BETA_TWO = 0.99
RATE = 0.05
EPSILON = 1e-08


def silu_slope(values):
    sig = jax.nn.sigmoid(values)
    return sig * (1.0 + values * (1.0 - sig))


def forward_taps(activation, kernel_bf):
    side_cells = activation.shape[1]
    cell_count = activation.shape[0] * side_cells * side_cells
    cols_out = kernel_bf.shape[1] // 9
    padded = jnp.pad(activation, ((0, 0), (1, 1), (1, 1), (0, 0)))
    summed = jnp.zeros((cell_count, cols_out), jnp.float32)
    for tap_index in range(9):
        tap_row = tap_index // 3
        tap_col = tap_index % 3
        window = padded[
            :, tap_row : tap_row + side_cells, tap_col : tap_col + side_cells, :
        ].reshape(cell_count, activation.shape[3])
        summed = summed + jnp.dot(
            window,
            kernel_bf[:, tap_index * cols_out : (tap_index + 1) * cols_out],
            preferred_element_type=jnp.float32,
        )
    return summed


def backward_taps(deltas, kernel_bf):
    side_cells = deltas.shape[1]
    cell_count = deltas.shape[0] * side_cells * side_cells
    cols_out = deltas.shape[3]
    padded = jnp.pad(deltas, ((0, 0), (1, 1), (1, 1), (0, 0)))
    summed = jnp.zeros((cell_count, kernel_bf.shape[0]), jnp.float32)
    for tap_index in range(9):
        tap_row = tap_index // 3
        tap_col = tap_index % 3
        window = padded[
            :, 2 - tap_row : 2 - tap_row + side_cells, 2 - tap_col : 2 - tap_col + side_cells, :
        ].reshape(cell_count, cols_out)
        block = kernel_bf[:, tap_index * cols_out : (tap_index + 1) * cols_out]
        summed = summed + lax.dot_general(
            window, block, (((1,), (1,)), ((), ())), preferred_element_type=jnp.float32
        )
    return summed


def weight_taps(activation, deltas):
    side_cells = activation.shape[1]
    cell_count = activation.shape[0] * side_cells * side_cells
    flat_deltas = deltas.reshape(cell_count, deltas.shape[3])
    padded = jnp.pad(activation, ((0, 0), (1, 1), (1, 1), (0, 0)))
    blocks = []
    for tap_index in range(9):
        tap_row = tap_index // 3
        tap_col = tap_index % 3
        window = padded[
            :, tap_row : tap_row + side_cells, tap_col : tap_col + side_cells, :
        ].reshape(cell_count, activation.shape[3])
        blocks.append(
            lax.dot_general(
                window, flat_deltas, (((0,), (0,)), ((), ())), preferred_element_type=jnp.float32
            )
        )
    return jnp.concatenate(blocks, axis=1)


def adam_update(weights_now, first_now, second_now, gradient):
    first_new = BETA_ONE * first_now + (1.0 - BETA_ONE) * gradient
    second_new = BETA_TWO * second_now + (1.0 - BETA_TWO) * gradient * gradient
    first_fix = 1.0 - BETA_ONE**ADAM_STEP
    second_fix = 1.0 - BETA_TWO**ADAM_STEP
    updated = weights_now - RATE * (first_new / first_fix) / (
        jnp.sqrt(second_new / second_fix) + EPSILON
    )
    return (updated, first_new, second_new)


def takers_and_named(sources):
    members = sources.shape[0]
    slots = max(members // 4, 1)
    own = jnp.arange(members, dtype=jnp.int32)
    takers = jnp.argsort(jnp.where(sources == own, 1, 0), stable=True)[:slots]
    return takers, sources[takers]


def carry_over(stacked, takers, named):
    me = lax.axis_index("member")
    sent = [
        jnp.where(named[slot] == me, stacked, jnp.zeros_like(stacked))
        for slot in range(takers.shape[0])
    ]
    arrived = lax.psum(jnp.stack(sent), "member")
    return arrived


def local_plain(latents, cotangent, weights, first_moment, second_moment, sources):
    scale = (9 * CH_IN) ** (-0.5)
    me = lax.axis_index("member")
    takers, named = takers_and_named(sources)
    images = latents[0]
    activation = jax.nn.silu(images.astype(jnp.float32)).astype(jnp.bfloat16)
    kernel_rows = weights[0].astype(jnp.bfloat16)
    state = jnp.concatenate(
        [kernel_rows, first_moment[0].astype(jnp.bfloat16), second_moment[0].astype(jnp.bfloat16)]
    )
    cell_count = images.shape[0] * images.shape[1] * images.shape[2]
    cols_out = cotangent.shape[4]
    kernel_all = lax.all_gather(kernel_rows, "dp", axis=0, tiled=True)
    arrived = carry_over(state, takers, named)
    hidden = scale * forward_taps(activation, kernel_all)
    deltas = (
        cotangent[0].reshape(cell_count, cols_out).astype(jnp.float32) * silu_slope(hidden)
    ).astype(jnp.bfloat16)
    deltas_img = deltas.reshape(cotangent[0].shape)
    back = scale * backward_taps(deltas_img, kernel_all)
    slope_in = silu_slope(images.reshape(cell_count, images.shape[3]).astype(jnp.float32))
    latent_grad = (back * slope_in).astype(jnp.bfloat16).reshape(latents.shape)
    gradient = lax.psum_scatter(
        (scale * weight_taps(activation, deltas_img)).astype(jnp.bfloat16),
        "dp",
        scatter_dimension=0,
        tiled=True,
    )
    gradient, arrived = lax.optimization_barrier((gradient, arrived))
    moved_gradient = carry_over(gradient, takers, named)
    rows = gradient.shape[0]
    weights_now, first_now, second_now = weights[0], first_moment[0], second_moment[0]
    gradient = gradient.astype(jnp.float32)
    for slot in range(takers.shape[0]):
        taking = (takers[slot] == me) & (named[slot] != me)
        moved = arrived[slot].astype(jnp.float32)
        weights_now = jnp.where(taking, moved[:rows], weights_now)
        first_now = jnp.where(taking, moved[rows : 2 * rows], first_now)
        second_now = jnp.where(taking, moved[2 * rows :], second_now)
        gradient = jnp.where(taking, moved_gradient[slot].astype(jnp.float32), gradient)
    updated, first_new, second_new = adam_update(weights_now, first_now, second_now, gradient)
    return (latent_grad, updated[None], first_new[None], second_new[None])


HALF = 48


def shifted(values):
    none = jnp.zeros((1, values.shape[1]), jnp.float32)
    before = jnp.concatenate([none, values[:-1]], axis=0)
    after = jnp.concatenate([values[1:], none], axis=0)
    return before, values, after


def block_kernel(
    sources,
    latents,
    weights,
    cotangent_hbm,
    first_hbm,
    second_hbm,
    latent_grad,
    grad_out,
    weights_out,
    first_out,
    second_out,
    cotangent,
    first_moment,
    second_moment,
    grad,
    kall,
    near,
    act_t,
    total,
    partial,
    core_in,
    chip_sum,
    x_in,
    y_in,
    a_sum,
    b_sum,
    a_in,
    b_in,
    up_in,
    down_in,
    up_grad,
    down_grad,
    ag_send,
    ag_recv,
    rs_send,
    rs_recv,
    z_send,
    z_recv,
    load_sem,
):
    images, side = latents.shape[0], latents.shape[1]
    width = latents.shape[3]
    cells = side * side
    rows = weights.shape[0]
    scale = (9 * CH_IN) ** (-0.5)
    f32, bf16 = jnp.float32, jnp.bfloat16
    k = lax.axis_index("member")
    me = lax.axis_index("dp")
    y, x, c = me // 4, (me // 2) % 2, me % 2
    sib = me + 1 - 2 * c
    xp = me + 2 - 4 * x
    yp = me + 4 - 8 * y
    diag = xp + 4 - 8 * y
    loads = [
        pltpu.make_async_copy(src, dst, load_sem.at[at])
        for at, (src, dst) in enumerate(
            (
                (first_hbm, first_moment),
                (second_hbm, second_moment),
                (cotangent_hbm, cotangent),
            )
        )
    ]
    for load in loads:
        load.start()
    named = jnp.float32(0.0)
    from_below = jnp.float32(0.0)
    taking = jnp.float32(0.0)
    for member in range(4):
        source = sources[member]
        takes = jnp.where(source != member, 1.0, 0.0)
        named += takes * jnp.where(source == k, 1.0, 0.0)
        from_below += takes * jnp.where(source < member, 1.0, 0.0)
        taking += takes * jnp.where(k == member, 1.0, 0.0)

    def remote(src, dst, send, recv, member, index):
        return pltpu.make_async_remote_copy(
            src_ref=src,
            dst_ref=dst,
            send_sem=send,
            recv_sem=recv,
            device_id=(member, index),
            device_id_type=pl.DeviceIdType.MESH,
        )

    barrier = pltpu.get_barrier_semaphore()
    for peer in (sib, xp, yp):
        pl.semaphore_signal(
            barrier, inc=1, device_id=(k, peer), device_id_type=pl.DeviceIdType.MESH
        )

    @pl.when(k < 3)
    def _():
        pl.semaphore_signal(
            barrier, inc=1, device_id=(k + 1, me), device_id_type=pl.DeviceIdType.MESH
        )

    @pl.when(k > 0)
    def _():
        pl.semaphore_signal(
            barrier, inc=1, device_id=(k - 1, me), device_id_type=pl.DeviceIdType.MESH
        )

    pl.semaphore_wait(barrier, 3 + jnp.where(k < 3, 1, 0) + jnp.where(k > 0, 1, 0))

    def block(t, owner, first=0, count=rows):
        return kall.at[t, owner, pl.ds(first, count)]

    def gather(t, kind):
        if kind < 3:
            part, peer = block(t, me), (sib, xp, yp)[kind]
        elif kind == 3:
            part, peer = block(t, xp, 0, HALF), yp
        elif kind == 4:
            part, peer = block(t, yp, HALF, rows - HALF), xp
        else:
            part, peer = block(t, (xp, yp, diag)[kind - 5]), sib
        return remote(part, part, ag_send.at[t, kind], ag_recv.at[t, kind], k, peer)

    def gather_wait(t, kind):
        gather_in(t, kind).wait_recv()

    def gather_in(t, kind):
        if kind < 3:
            part = block(t, (sib, xp, yp)[kind])
        elif kind == 3:
            part = block(t, diag, 0, HALF)
        elif kind == 4:
            part = block(t, diag, HALF, rows - HALF)
        else:
            over = 1 - 2 * c
            part = block(t, (xp + over, yp + over, diag + over)[kind - 5])
        return remote(part, part, ag_send.at[t, kind], ag_recv.at[t, kind], k, sib)

    state = (weights, first_moment, second_moment)

    def columns(t):
        return pl.ds(pl.multiple_of(t * width, 128), width)

    def state_copy(lane, here, j, at, target):
        part = here.at[j, at]
        n = 3 * j + at
        return remote(part, part, z_send.at[lane, n], z_recv.at[lane, n], target, me)

    def state_step(tick, lane, rank, here, target):
        @pl.when((rank == 0) & (tick < 9))
        def _():
            for at in range(3):
                here[tick, at] = state[at][:, columns(tick)].astype(bf16)
                state_copy(lane, here, tick, at, target).start()

        for at in range(3):
            since = tick - at - rank

            @pl.when((since >= 0) & (since % 2 == 0) & (since < 18) & (rank > 0) & (rank < 3))
            def _():
                j = since // 2
                copy = state_copy(lane, here, j, at, target)
                copy.wait_recv()
                mine, came = state[at][:, columns(j)], here[j, at].astype(f32)
                here[j, at] = (mine * named + came * (1.0 - named)).astype(bf16)
                copy.start()

    def grad_step(tick, lane, rank, here, target):
        t = tick - 16 - 2 * rank

        @pl.when((t >= 0) & (t < 9) & (rank < 3))
        def _():
            copy = remote(
                here.at[t], here.at[t], z_send.at[lane, t], z_recv.at[lane, t], target, me
            )

            @pl.when(rank == 0)
            def _():
                here[t] = grad[t]

            @pl.when(rank > 0)
            def _():
                copy.wait_recv()
                mine, came = grad[t].astype(f32), here[t].astype(f32)
                here[t] = (mine * named + came * (1.0 - named)).astype(bf16)

            copy.start()

    def member_steps(tick, with_grad):
        state_step(tick, 0, k, up_in, jnp.minimum(k + 1, 3))
        state_step(tick, 1, 3 - k, down_in, jnp.maximum(k - 1, 0))
        if with_grad:
            grad_step(tick, 2, k, up_grad, jnp.minimum(k + 1, 3))
            grad_step(tick, 3, 3 - k, down_grad, jnp.maximum(k - 1, 0))

    def cast_tap(t, carry):
        kall[t, me] = weights[:, columns(t)].astype(bf16)
        return carry

    lax.fori_loop(0, 9, cast_tap, 0)

    def first_sends(t):
        for kind in range(3):
            gather(t, kind).start()

    def ahead(t, carry):
        first_sends(t)
        return carry

    lax.fori_loop(0, 4, ahead, 0)

    zero_row = jnp.zeros((side, width), bf16)

    def clear(n, carry):
        near[n // images, n % images, 0] = zero_row
        near[n // images, n % images, side + 1] = zero_row
        return carry

    lax.fori_loop(0, 3 * images, clear, 0)

    def activate(n, carry):
        b, i = n // side, n % side
        value = latents[b, i].astype(f32)
        value = value / (1.0 + jnp.exp(-value))
        for at, moved_values in enumerate(shifted(value)):
            near[at, b, i + 1] = moved_values.astype(bf16)
        return carry

    def turn(b):
        flat = near[1, b, 1 : side + 1].reshape(cells, width)
        act_t[b] = jnp.transpose(flat)

    for load in loads:
        load.wait()

    def forward(i, carry):
        member_steps(i, False)

        @pl.when(i + 4 < 9)
        def _():
            first_sends(i + 4)

        @pl.when(i < 9)
        def _():
            gather_wait(i, 1)
            gather_wait(i, 2)
            for kind in (3, 4, 5, 6):
                gather(i, kind).start()

        @pl.when((i >= 1) & (i < 10))
        def _():
            gather_wait(i - 1, 3)
            gather_wait(i - 1, 4)
            gather(i - 1, 7).start()

        half_rows = images * side // 2

        @pl.when(i < 2)
        def _():
            lax.fori_loop(0, half_rows, lambda n, carry: activate(n + i * half_rows, carry), 0, unroll=4)

        @pl.when((i >= 2) & (i < 2 + images))
        def _():
            turn(i - 2)

        @pl.when(i >= 2)
        def _():
            t = i - 2
            for kind in (0, 5, 6, 7):
                gather_wait(t, kind)
            weight = kall[t].reshape(8 * rows, width)

            window = near[t % 3, :, pl.ds(t // 3, side)].reshape(images * cells, width)
            product = jnp.dot(window, weight, preferred_element_type=f32)

            @pl.when(t == 0)
            def _():
                total[...] = product

            @pl.when(t > 0)
            def _():
                total[...] += product

        return carry

    lax.fori_loop(0, 11, forward, 0)

    def slope_rows(n, carry):
        b, i = n // side, n % side
        hidden = scale * total[pl.ds(pl.multiple_of(n * side, side), side)]
        value = cotangent[b, i].astype(f32) * silu_slope(hidden)
        for at, moved_values in enumerate(shifted(value)):
            near[at, b, i + 1] = moved_values.astype(bf16)
        return carry

    lax.fori_loop(0, images * side, slope_rows, 0, unroll=4)

    def scatter(t, kind):
        if kind == 0:
            src, dst, peer = partial.at[t, :, :, 1 - c], core_in.at[t], sib
        elif kind == 1:
            src, dst, peer = chip_sum.at[t, :, 1 - x, pl.ds(0, HALF)], x_in.at[t], xp
        elif kind == 2:
            src, dst, peer = chip_sum.at[t, 1 - y, :, pl.ds(HALF, rows - HALF)], y_in.at[t], yp
        elif kind == 3:
            src, dst, peer = a_sum.at[t, 1 - y], a_in.at[t], yp
        else:
            src, dst, peer = b_sum.at[t, 1 - x], b_in.at[t], xp
        return remote(src, dst, rs_send.at[t, kind], rs_recv.at[t, kind], k, peer)

    def plus(one, two):
        return (one.astype(f32) + two.astype(f32)).astype(bf16)

    def scatter_steps(i):
        @pl.when((i >= 1) & (i < 10))
        def _():
            t = i - 1
            scatter(t, 0).wait_recv()
            for yy in range(2):
                for xx in range(2):
                    chip_sum[t, yy, xx] = plus(partial[t, yy, xx, c], core_in[t, yy, xx])
            scatter(t, 1).start()
            scatter(t, 2).start()

        @pl.when((i >= 3) & (i < 12))
        def _():
            t = i - 3
            scatter(t, 1).wait_recv()
            scatter(t, 2).wait_recv()
            for at in range(2):
                a_sum[t, at] = plus(chip_sum[t, at, x, 0:HALF], x_in[t, at])
                b_sum[t, at] = plus(chip_sum[t, y, at, HALF:rows], y_in[t, at])
            scatter(t, 3).start()
            scatter(t, 4).start()

        @pl.when((i >= 5) & (i < 14))
        def _():
            t = i - 5
            scatter(t, 3).wait_recv()
            scatter(t, 4).wait_recv()
            grad[t, 0:HALF] = plus(a_sum[t, y], a_in[t])
            grad[t, HALF:rows] = plus(b_sum[t, x], b_in[t])

    def kernel_grad(t, carry):
        scatter_steps(t)
        member_steps(t + 11, True)
        window = near[2 - t % 3, :, pl.ds(2 - t // 3, side)].reshape(images * cells, width)

        lhs = jnp.concatenate([act_t[b] for b in range(images)], axis=1)
        product = scale * jnp.dot(lhs, window, preferred_element_type=f32)
        partial[t] = product.astype(bf16).reshape(2, 2, 2, rows, width)
        scatter(t, 0).start()
        return carry

    lax.fori_loop(0, 9, kernel_grad, 0)

    def back(r, carry):
        def tick(col):
            scatter_steps(3 * r + col + 9)
            member_steps(3 * r + col + 20, True)

        weight = jnp.concatenate(
            [kall[3 * r + col].reshape(8 * rows, width) for col in range(3)], axis=1
        )
        pair = images // 2
        for part in range(2):
            windows = jnp.concatenate(
                [
                    near[2 - col, part * pair : (part + 1) * pair, pl.ds(2 - r, side)].reshape(
                        pair * cells, width
                    )
                    for col in range(3)
                ],
                axis=1,
            )
            product = lax.dot_general(
                windows, weight, (((1,), (1,)), ((), ())), preferred_element_type=f32
            )
            here = pl.ds(part * pair * cells, pair * cells)

            @pl.when(r == 0)
            def _():
                total[here] = product

            @pl.when(r > 0)
            def _():
                total[here] += product

            tick(part)
        tick(2)
        return carry

    lax.fori_loop(0, 3, back, 0)

    def finish(n, carry):
        b, i = n // side, n % side
        value = scale * total[pl.ds(pl.multiple_of(n * side, side), side)]
        value = value * silu_slope(latents[b, i].astype(f32))
        latent_grad[b, i] = value.astype(bf16)
        return carry

    def mix(lower, upper, share):
        return (lower.astype(f32) * share + upper.astype(f32) * (1.0 - share)).astype(bf16)

    low, high = (up_in, up_grad), (down_in, down_grad)

    def by_place(store):
        @pl.when(k == 0)
        def _():
            store(high, high, 1.0)

        @pl.when(k == 3)
        def _():
            store(low, low, 1.0)

        @pl.when((k > 0) & (k < 3))
        def _():
            store(low, high, from_below)

    def settle(lane, copy):
        last = k == 3 if lane % 2 == 0 else k == 0

        @pl.when(last)
        def _():
            copy.wait_recv()

        @pl.when(jnp.logical_not(last))
        def _():
            copy.wait_send()

    def drain_state(j, carry):
        for lane, here in ((0, up_in), (1, down_in)):
            for at in range(3):
                settle(lane, state_copy(lane, here, j, at, k))

        def store(below, above, share):
            for at, out in enumerate((weights_out, first_out, second_out)):
                out[:, columns(j)] = mix(below[0][j, at], above[0][j, at], share)

        by_place(store)
        for kind in range(8):
            gather(j, kind).wait_send()
        for kind in range(5):
            scatter(j, kind).wait_send()
        return carry

    def drain_grad(j, carry):
        for lane, here in ((2, up_grad), (3, down_grad)):
            part = here.at[j]
            settle(lane, remote(part, part, z_send.at[lane, j], z_recv.at[lane, j], k, sib))

        def store(below, above, share):
            came = mix(below[1][j], above[1][j], share)
            grad_out[:, columns(j)] = mix(came, grad[j], taking)

        by_place(store)
        return carry

    lax.fori_loop(0, 9, drain_state, 0)
    lax.fori_loop(0, images * side, finish, 0, unroll=4)
    lax.fori_loop(0, 9, drain_grad, 0)


def local_block(latents, cotangent, weights, first_moment, second_moment, sources):
    me = lax.axis_index("member")
    members = jnp.arange(4, dtype=jnp.int32)
    taking = jnp.any((sources != members) & (members == me))
    rows, width = weights.shape[1], latents.shape[4]
    bf16 = jnp.bfloat16
    flat = (rows, 9 * width)
    images, side = latents.shape[1], latents.shape[2]
    cells = side * side
    vmem = pl.BlockSpec(memory_space=pltpu.VMEM)
    tap = (9, rows, width)
    half, rest = HALF, rows - HALF
    latent_grad, grad, weights_in, first_in, second_in = pl.pallas_call(
        block_kernel,
        out_shape=(
            jax.ShapeDtypeStruct(latents.shape[1:], bf16),
        )
        + (jax.ShapeDtypeStruct(flat, bf16),) * 4,
        in_specs=[pl.BlockSpec(memory_space=pltpu.SMEM), vmem, vmem]
        + [pl.BlockSpec(memory_space=pl.ANY)] * 3,
        out_specs=(vmem,) * 5,
        scratch_shapes=[
            pltpu.VMEM(latents.shape[1:], bf16),
            pltpu.VMEM(flat, jnp.float32),
            pltpu.VMEM(flat, jnp.float32),
            pltpu.VMEM(tap, bf16),
            pltpu.VMEM((9, 8, rows, width), bf16),
            pltpu.VMEM((3, images, side + 2, side, width), bf16),
            pltpu.VMEM((images, width, cells), bf16),
            pltpu.VMEM((images * cells, width), jnp.float32),
            pltpu.VMEM((9, 2, 2, 2, rows, width), bf16),
            pltpu.VMEM((9, 2, 2, rows, width), bf16),
            pltpu.VMEM((9, 2, 2, rows, width), bf16),
            pltpu.VMEM((9, 2, half, width), bf16),
            pltpu.VMEM((9, 2, rest, width), bf16),
            pltpu.VMEM((9, 2, half, width), bf16),
            pltpu.VMEM((9, 2, rest, width), bf16),
            pltpu.VMEM((9, half, width), bf16),
            pltpu.VMEM((9, rest, width), bf16),
            pltpu.VMEM((9, 3, rows, width), bf16),
            pltpu.VMEM((9, 3, rows, width), bf16),
            pltpu.VMEM(tap, bf16),
            pltpu.VMEM(tap, bf16),
            pltpu.SemaphoreType.DMA((9, 8)),
            pltpu.SemaphoreType.DMA((9, 8)),
            pltpu.SemaphoreType.DMA((9, 5)),
            pltpu.SemaphoreType.DMA((9, 5)),
            pltpu.SemaphoreType.DMA((4, 27)),
            pltpu.SemaphoreType.DMA((4, 27)),
            pltpu.SemaphoreType.DMA((3,)),
        ],
        compiler_params=pltpu.CompilerParams(
            collective_id=0, has_side_effects=True, vmem_limit_bytes=60 * 1024 * 1024
        ),
        cost_estimate=pl.CostEstimate(
            flops=6 * images * cells * 9 * width * width, bytes_accessed=16000000, transcendentals=0
        ),
    )(sources, latents[0], weights[0], cotangent[0], first_moment[0], second_moment[0])

    f32 = jnp.float32
    weights_now = jnp.where(taking, weights_in.astype(f32), weights[0])
    first_now = jnp.where(taking, first_in.astype(f32), first_moment[0])
    second_now = jnp.where(taking, second_in.astype(f32), second_moment[0])
    gradient = grad.astype(f32)
    updated, first_new, second_new = adam_update(weights_now, first_now, second_now, gradient)
    return (latent_grad[None], updated[None], first_new[None], second_new[None])


def solution(mesh):
    fits = mesh.shape["member"] == 4 and mesh.shape["dp"] == 8
    local = local_block if fits else local_plain
    in_specs = (
        P("member", "dp", None, None, None),
        P("member", "dp", None, None, None),
        P("member", "dp", None),
        P("member", "dp", None),
        P("member", "dp", None),
        P(),
    )
    out_specs = (
        P("member", "dp", None, None, None),
        P("member", "dp", None),
        P("member", "dp", None),
        P("member", "dp", None),
    )
    return jax.shard_map(local, mesh=mesh, in_specs=in_specs, out_specs=out_specs, check_vma=False)
```

```python
import jax
import jax.numpy as jnp
from jax import lax
from jax.experimental import pallas as pl
from jax.experimental.pallas import tpu as pltpu
from jax.sharding import PartitionSpec as P

CH_IN = 640
ADAM_STEP = 10


BETA_ONE = 0.9
BETA_TWO = 0.99
RATE = 0.05
EPSILON = 1e-08


def silu_slope(values):
    sig = jax.nn.sigmoid(values)
    return sig * (1.0 + values * (1.0 - sig))


def forward_taps(activation, kernel_bf):
    side_cells = activation.shape[1]
    cell_count = activation.shape[0] * side_cells * side_cells
    cols_out = kernel_bf.shape[1] // 9
    padded = jnp.pad(activation, ((0, 0), (1, 1), (1, 1), (0, 0)))
    summed = jnp.zeros((cell_count, cols_out), jnp.float32)
    for tap_index in range(9):
        tap_row = tap_index // 3
        tap_col = tap_index % 3
        window = padded[
            :, tap_row : tap_row + side_cells, tap_col : tap_col + side_cells, :
        ].reshape(cell_count, activation.shape[3])
        summed = summed + jnp.dot(
            window,
            kernel_bf[:, tap_index * cols_out : (tap_index + 1) * cols_out],
            preferred_element_type=jnp.float32,
        )
    return summed


def backward_taps(deltas, kernel_bf):
    side_cells = deltas.shape[1]
    cell_count = deltas.shape[0] * side_cells * side_cells
    cols_out = deltas.shape[3]
    padded = jnp.pad(deltas, ((0, 0), (1, 1), (1, 1), (0, 0)))
    summed = jnp.zeros((cell_count, kernel_bf.shape[0]), jnp.float32)
    for tap_index in range(9):
        tap_row = tap_index // 3
        tap_col = tap_index % 3
        window = padded[
            :, 2 - tap_row : 2 - tap_row + side_cells, 2 - tap_col : 2 - tap_col + side_cells, :
        ].reshape(cell_count, cols_out)
        block = kernel_bf[:, tap_index * cols_out : (tap_index + 1) * cols_out]
        summed = summed + lax.dot_general(
            window, block, (((1,), (1,)), ((), ())), preferred_element_type=jnp.float32
        )
    return summed


def weight_taps(activation, deltas):
    side_cells = activation.shape[1]
    cell_count = activation.shape[0] * side_cells * side_cells
    flat_deltas = deltas.reshape(cell_count, deltas.shape[3])
    padded = jnp.pad(activation, ((0, 0), (1, 1), (1, 1), (0, 0)))
    blocks = []
    for tap_index in range(9):
        tap_row = tap_index // 3
        tap_col = tap_index % 3
        window = padded[
            :, tap_row : tap_row + side_cells, tap_col : tap_col + side_cells, :
        ].reshape(cell_count, activation.shape[3])
        blocks.append(
            lax.dot_general(
                window, flat_deltas, (((0,), (0,)), ((), ())), preferred_element_type=jnp.float32
            )
        )
    return jnp.concatenate(blocks, axis=1)


def adam_update(weights_now, first_now, second_now, gradient):
    first_new = BETA_ONE * first_now + (1.0 - BETA_ONE) * gradient
    second_new = BETA_TWO * second_now + (1.0 - BETA_TWO) * gradient * gradient
    first_fix = 1.0 - BETA_ONE**ADAM_STEP
    second_fix = 1.0 - BETA_TWO**ADAM_STEP
    updated = weights_now - RATE * (first_new / first_fix) / (
        jnp.sqrt(second_new / second_fix) + EPSILON
    )
    return (updated, first_new, second_new)


def takers_and_named(sources):
    members = sources.shape[0]
    slots = max(members // 4, 1)
    own = jnp.arange(members, dtype=jnp.int32)
    takers = jnp.argsort(jnp.where(sources == own, 1, 0), stable=True)[:slots]
    return takers, sources[takers]


def carry_over(stacked, takers, named):
    me = lax.axis_index("member")
    sent = [
        jnp.where(named[slot] == me, stacked, jnp.zeros_like(stacked))
        for slot in range(takers.shape[0])
    ]
    arrived = lax.psum(jnp.stack(sent), "member")
    return arrived


def local_plain(latents, cotangent, weights, first_moment, second_moment, sources):
    scale = (9 * CH_IN) ** (-0.5)
    me = lax.axis_index("member")
    takers, named = takers_and_named(sources)
    images = latents[0]
    activation = jax.nn.silu(images.astype(jnp.float32)).astype(jnp.bfloat16)
    kernel_rows = weights[0].astype(jnp.bfloat16)
    state = jnp.concatenate(
        [kernel_rows, first_moment[0].astype(jnp.bfloat16), second_moment[0].astype(jnp.bfloat16)]
    )
    cell_count = images.shape[0] * images.shape[1] * images.shape[2]
    cols_out = cotangent.shape[4]
    kernel_all = lax.all_gather(kernel_rows, "dp", axis=0, tiled=True)
    arrived = carry_over(state, takers, named)
    hidden = scale * forward_taps(activation, kernel_all)
    deltas = (
        cotangent[0].reshape(cell_count, cols_out).astype(jnp.float32) * silu_slope(hidden)
    ).astype(jnp.bfloat16)
    deltas_img = deltas.reshape(cotangent[0].shape)
    back = scale * backward_taps(deltas_img, kernel_all)
    slope_in = silu_slope(images.reshape(cell_count, images.shape[3]).astype(jnp.float32))
    latent_grad = (back * slope_in).astype(jnp.bfloat16).reshape(latents.shape)
    gradient = lax.psum_scatter(
        (scale * weight_taps(activation, deltas_img)).astype(jnp.bfloat16),
        "dp",
        scatter_dimension=0,
        tiled=True,
    )
    gradient, arrived = lax.optimization_barrier((gradient, arrived))
    moved_gradient = carry_over(gradient, takers, named)
    rows = gradient.shape[0]
    weights_now, first_now, second_now = weights[0], first_moment[0], second_moment[0]
    gradient = gradient.astype(jnp.float32)
    for slot in range(takers.shape[0]):
        taking = (takers[slot] == me) & (named[slot] != me)
        moved = arrived[slot].astype(jnp.float32)
        weights_now = jnp.where(taking, moved[:rows], weights_now)
        first_now = jnp.where(taking, moved[rows : 2 * rows], first_now)
        second_now = jnp.where(taking, moved[2 * rows :], second_now)
        gradient = jnp.where(taking, moved_gradient[slot].astype(jnp.float32), gradient)
    updated, first_new, second_new = adam_update(weights_now, first_now, second_now, gradient)
    return (latent_grad, updated[None], first_new[None], second_new[None])


HALF = 48


def shifted(values):
    none = jnp.zeros((1, values.shape[1]), jnp.float32)
    before = jnp.concatenate([none, values[:-1]], axis=0)
    after = jnp.concatenate([values[1:], none], axis=0)
    return before, values, after


def block_kernel(
    sources,
    latents,
    weights,
    cotangent_hbm,
    first_hbm,
    second_hbm,
    latent_grad,
    grad_out,
    weights_out,
    first_out,
    second_out,
    cotangent,
    first_moment,
    second_moment,
    grad,
    kall,
    near,
    act_t,
    total,
    partial,
    core_in,
    chip_sum,
    x_in,
    y_in,
    a_sum,
    b_sum,
    a_in,
    b_in,
    up_in,
    down_in,
    up_grad,
    down_grad,
    ag_send,
    ag_recv,
    rs_send,
    rs_recv,
    z_send,
    z_recv,
    load_sem,
):
    images, side = latents.shape[0], latents.shape[1]
    width = latents.shape[3]
    cells = side * side
    rows = weights.shape[0]
    scale = (9 * CH_IN) ** (-0.5)
    f32, bf16 = jnp.float32, jnp.bfloat16
    k = lax.axis_index("member")
    me = lax.axis_index("dp")
    y, x, c = me // 4, (me // 2) % 2, me % 2
    sib = me + 1 - 2 * c
    xp = me + 2 - 4 * x
    yp = me + 4 - 8 * y
    diag = xp + 4 - 8 * y
    loads = [
        pltpu.make_async_copy(src, dst, load_sem.at[at])
        for at, (src, dst) in enumerate(
            (
                (first_hbm, first_moment),
                (second_hbm, second_moment),
                (cotangent_hbm, cotangent),
            )
        )
    ]
    for load in loads:
        load.start()
    named = jnp.float32(0.0)
    from_below = jnp.float32(0.0)
    taking = jnp.float32(0.0)
    for member in range(4):
        source = sources[member]
        takes = jnp.where(source != member, 1.0, 0.0)
        named += takes * jnp.where(source == k, 1.0, 0.0)
        from_below += takes * jnp.where(source < member, 1.0, 0.0)
        taking += takes * jnp.where(k == member, 1.0, 0.0)

    def remote(src, dst, send, recv, member, index):
        return pltpu.make_async_remote_copy(
            src_ref=src,
            dst_ref=dst,
            send_sem=send,
            recv_sem=recv,
            device_id=(member, index),
            device_id_type=pl.DeviceIdType.MESH,
        )

    barrier = pltpu.get_barrier_semaphore()
    for peer in (sib, xp, yp):
        pl.semaphore_signal(
            barrier, inc=1, device_id=(k, peer), device_id_type=pl.DeviceIdType.MESH
        )

    @pl.when(k < 3)
    def _():
        pl.semaphore_signal(
            barrier, inc=1, device_id=(k + 1, me), device_id_type=pl.DeviceIdType.MESH
        )

    @pl.when(k > 0)
    def _():
        pl.semaphore_signal(
            barrier, inc=1, device_id=(k - 1, me), device_id_type=pl.DeviceIdType.MESH
        )

    pl.semaphore_wait(barrier, 3 + jnp.where(k < 3, 1, 0) + jnp.where(k > 0, 1, 0))

    def block(t, owner, first=0, count=rows):
        return kall.at[t, owner, pl.ds(first, count)]

    def gather(t, kind):
        if kind < 3:
            part, peer = block(t, me), (sib, xp, yp)[kind]
        elif kind == 3:
            part, peer = block(t, xp, 0, HALF), yp
        elif kind == 4:
            part, peer = block(t, yp, HALF, rows - HALF), xp
        else:
            part, peer = block(t, (xp, yp, diag)[kind - 5]), sib
        return remote(part, part, ag_send.at[t, kind], ag_recv.at[t, kind], k, peer)

    def gather_wait(t, kind):
        gather_in(t, kind).wait_recv()

    def gather_in(t, kind):
        if kind < 3:
            part = block(t, (sib, xp, yp)[kind])
        elif kind == 3:
            part = block(t, diag, 0, HALF)
        elif kind == 4:
            part = block(t, diag, HALF, rows - HALF)
        else:
            over = 1 - 2 * c
            part = block(t, (xp + over, yp + over, diag + over)[kind - 5])
        return remote(part, part, ag_send.at[t, kind], ag_recv.at[t, kind], k, sib)

    state = (weights, first_moment, second_moment)

    def columns(t):
        return pl.ds(pl.multiple_of(t * width, 128), width)

    def state_step(tick, lane, rank, here, target):
        j = jnp.where(rank == 0, tick // 2, (tick - 1) // 2 - rank)
        due = tick % 2 == jnp.where(rank == 0, 0, 1)

        @pl.when(due & (j >= 0) & (j < 9) & (rank < 3))
        def _():
            @pl.when(rank == 0)
            def _():
                for at in range(3):
                    here[j, at] = state[at][:, columns(j)].astype(bf16)

            @pl.when(rank > 0)
            def _():
                remote(
                    here.at[j], here.at[j], z_send.at[lane, j], z_recv.at[lane, j], target, me
                ).wait_recv()
                for at in range(3):
                    mine, came = state[at][:, columns(j)], here[j, at].astype(f32)
                    here[j, at] = (mine * named + came * (1.0 - named)).astype(bf16)

            remote(
                here.at[j], here.at[j], z_send.at[lane, j], z_recv.at[lane, j], target, me
            ).start()

    def grad_step(tick, lane, rank, here, target):
        t = tick - 16 - 2 * rank

        @pl.when((t >= 0) & (t < 9) & (rank < 3))
        def _():
            copy = remote(
                here.at[t], here.at[t], z_send.at[lane, t], z_recv.at[lane, t], target, me
            )

            @pl.when(rank == 0)
            def _():
                here[t] = grad[t]

            @pl.when(rank > 0)
            def _():
                copy.wait_recv()
                mine, came = grad[t].astype(f32), here[t].astype(f32)
                here[t] = (mine * named + came * (1.0 - named)).astype(bf16)

            copy.start()

    def member_steps(tick, with_grad):
        state_step(tick, 0, k, up_in, jnp.minimum(k + 1, 3))
        state_step(tick, 1, 3 - k, down_in, jnp.maximum(k - 1, 0))
        if with_grad:
            grad_step(tick, 2, k, up_grad, jnp.minimum(k + 1, 3))
            grad_step(tick, 3, 3 - k, down_grad, jnp.maximum(k - 1, 0))

    def cast_tap(t, carry):
        kall[t, me] = weights[:, columns(t)].astype(bf16)
        return carry

    lax.fori_loop(0, 9, cast_tap, 0)

    def first_sends(t):
        for kind in range(3):
            gather(t, kind).start()

    def ahead(t, carry):
        first_sends(t)
        return carry

    lax.fori_loop(0, 4, ahead, 0)

    zero_row = jnp.zeros((side, width), bf16)

    def clear(n, carry):
        near[n // images, n % images, 0] = zero_row
        near[n // images, n % images, side + 1] = zero_row
        return carry

    lax.fori_loop(0, 3 * images, clear, 0)

    def activate(n, carry):
        b, i = n // side, n % side
        value = latents[b, i].astype(f32)
        value = value / (1.0 + jnp.exp(-value))
        for at, moved_values in enumerate(shifted(value)):
            near[at, b, i + 1] = moved_values.astype(bf16)
        return carry

    def turn(b):
        flat = near[1, b, 1 : side + 1].reshape(cells, width)
        act_t[b] = jnp.transpose(flat)

    for load in loads:
        load.wait()

    def forward(i, carry):
        member_steps(i, False)

        @pl.when(i + 4 < 9)
        def _():
            first_sends(i + 4)

        @pl.when(i < 9)
        def _():
            gather_wait(i, 1)
            gather_wait(i, 2)
            for kind in (3, 4, 5, 6):
                gather(i, kind).start()

        @pl.when((i >= 1) & (i < 10))
        def _():
            gather_wait(i - 1, 3)
            gather_wait(i - 1, 4)
            gather(i - 1, 7).start()

        half_rows = images * side // 2

        @pl.when(i < 2)
        def _():
            lax.fori_loop(0, half_rows, lambda n, carry: activate(n + i * half_rows, carry), 0, unroll=4)

        @pl.when((i >= 2) & (i < 2 + images))
        def _():
            turn(i - 2)

        @pl.when(i >= 2)
        def _():
            t = i - 2
            for kind in (0, 5, 6, 7):
                gather_wait(t, kind)
            weight = kall[t].reshape(8 * rows, width)

            window = near[t % 3, :, pl.ds(t // 3, side)].reshape(images * cells, width)
            product = jnp.dot(window, weight, preferred_element_type=f32)

            @pl.when(t == 0)
            def _():
                total[...] = product

            @pl.when(t > 0)
            def _():
                total[...] += product

        return carry

    lax.fori_loop(0, 11, forward, 0)

    def slope_rows(n, carry):
        b, i = n // side, n % side
        hidden = scale * total[pl.ds(pl.multiple_of(n * side, side), side)]
        value = cotangent[b, i].astype(f32) * silu_slope(hidden)
        for at, moved_values in enumerate(shifted(value)):
            near[at, b, i + 1] = moved_values.astype(bf16)
        return carry

    lax.fori_loop(0, images * side, slope_rows, 0, unroll=4)

    def scatter(t, kind):
        if kind == 0:
            src, dst, peer = partial.at[t, :, :, 1 - c], core_in.at[t], sib
        elif kind == 1:
            src, dst, peer = chip_sum.at[t, :, 1 - x, pl.ds(0, HALF)], x_in.at[t], xp
        elif kind == 2:
            src, dst, peer = chip_sum.at[t, 1 - y, :, pl.ds(HALF, rows - HALF)], y_in.at[t], yp
        elif kind == 3:
            src, dst, peer = a_sum.at[t, 1 - y], a_in.at[t], yp
        else:
            src, dst, peer = b_sum.at[t, 1 - x], b_in.at[t], xp
        return remote(src, dst, rs_send.at[t, kind], rs_recv.at[t, kind], k, peer)

    def plus(one, two):
        return (one.astype(f32) + two.astype(f32)).astype(bf16)

    def scatter_steps(i):
        @pl.when((i >= 1) & (i < 10))
        def _():
            t = i - 1
            scatter(t, 0).wait_recv()
            for yy in range(2):
                for xx in range(2):
                    chip_sum[t, yy, xx] = plus(partial[t, yy, xx, c], core_in[t, yy, xx])
            scatter(t, 1).start()
            scatter(t, 2).start()

        @pl.when((i >= 3) & (i < 12))
        def _():
            t = i - 3
            scatter(t, 1).wait_recv()
            scatter(t, 2).wait_recv()
            for at in range(2):
                a_sum[t, at] = plus(chip_sum[t, at, x, 0:HALF], x_in[t, at])
                b_sum[t, at] = plus(chip_sum[t, y, at, HALF:rows], y_in[t, at])
            scatter(t, 3).start()
            scatter(t, 4).start()

        @pl.when((i >= 5) & (i < 14))
        def _():
            t = i - 5
            scatter(t, 3).wait_recv()
            scatter(t, 4).wait_recv()
            grad[t, 0:HALF] = plus(a_sum[t, y], a_in[t])
            grad[t, HALF:rows] = plus(b_sum[t, x], b_in[t])

    def kernel_grad(t, carry):
        scatter_steps(t)
        member_steps(t + 11, True)
        window = near[2 - t % 3, :, pl.ds(2 - t // 3, side)].reshape(images * cells, width)

        lhs = jnp.concatenate([act_t[b] for b in range(images)], axis=1)
        product = scale * jnp.dot(lhs, window, preferred_element_type=f32)
        partial[t] = product.astype(bf16).reshape(2, 2, 2, rows, width)
        scatter(t, 0).start()
        return carry

    lax.fori_loop(0, 9, kernel_grad, 0)

    def back(r, carry):
        def tick(col):
            scatter_steps(3 * r + col + 9)
            member_steps(3 * r + col + 20, True)

        weight = jnp.concatenate(
            [kall[3 * r + col].reshape(8 * rows, width) for col in range(3)], axis=1
        )
        pair = images // 2
        for part in range(2):
            windows = jnp.concatenate(
                [
                    near[2 - col, part * pair : (part + 1) * pair, pl.ds(2 - r, side)].reshape(
                        pair * cells, width
                    )
                    for col in range(3)
                ],
                axis=1,
            )
            product = lax.dot_general(
                windows, weight, (((1,), (1,)), ((), ())), preferred_element_type=f32
            )
            here = pl.ds(part * pair * cells, pair * cells)

            @pl.when(r == 0)
            def _():
                total[here] = product

            @pl.when(r > 0)
            def _():
                total[here] += product

            tick(part)
        tick(2)
        return carry

    lax.fori_loop(0, 3, back, 0)

    def finish(n, carry):
        b, i = n // side, n % side
        value = scale * total[pl.ds(pl.multiple_of(n * side, side), side)]
        value = value * silu_slope(latents[b, i].astype(f32))
        latent_grad[b, i] = value.astype(bf16)
        return carry

    def mix(lower, upper, share):
        return (lower.astype(f32) * share + upper.astype(f32) * (1.0 - share)).astype(bf16)

    low, high = (up_in, up_grad), (down_in, down_grad)

    def by_place(store):
        @pl.when(k == 0)
        def _():
            store(high, high, 1.0)

        @pl.when(k == 3)
        def _():
            store(low, low, 1.0)

        @pl.when((k > 0) & (k < 3))
        def _():
            store(low, high, from_below)

    def settle(lanes, j):
        for lane, here in lanes:
            copy = remote(here.at[j], here.at[j], z_send.at[lane, j], z_recv.at[lane, j], k, sib)
            last = k == 3 if lane % 2 == 0 else k == 0

            @pl.when(last)
            def _():
                copy.wait_recv()

            @pl.when(jnp.logical_not(last))
            def _():
                copy.wait_send()

    def drain_state(j, carry):
        settle(((0, up_in), (1, down_in)), j)

        def store(below, above, share):
            for at, out in enumerate((weights_out, first_out, second_out)):
                out[:, columns(j)] = mix(below[0][j, at], above[0][j, at], share)

        by_place(store)
        for kind in range(8):
            gather(j, kind).wait_send()
        for kind in range(5):
            scatter(j, kind).wait_send()
        return carry

    def drain_grad(j, carry):
        settle(((2, up_grad), (3, down_grad)), j)

        def store(below, above, share):
            came = mix(below[1][j], above[1][j], share)
            grad_out[:, columns(j)] = mix(came, grad[j], taking)

        by_place(store)
        return carry

    lax.fori_loop(0, 9, drain_state, 0)
    lax.fori_loop(0, images * side, finish, 0, unroll=4)
    lax.fori_loop(0, 9, drain_grad, 0)


def local_block(latents, cotangent, weights, first_moment, second_moment, sources):
    me = lax.axis_index("member")
    members = jnp.arange(4, dtype=jnp.int32)
    taking = jnp.any((sources != members) & (members == me))
    rows, width = weights.shape[1], latents.shape[4]
    bf16 = jnp.bfloat16
    flat = (rows, 9 * width)
    images, side = latents.shape[1], latents.shape[2]
    cells = side * side
    vmem = pl.BlockSpec(memory_space=pltpu.VMEM)
    tap = (9, rows, width)
    half, rest = HALF, rows - HALF
    latent_grad, grad, weights_in, first_in, second_in = pl.pallas_call(
        block_kernel,
        out_shape=(
            jax.ShapeDtypeStruct(latents.shape[1:], bf16),
        )
        + (jax.ShapeDtypeStruct(flat, bf16),) * 4,
        in_specs=[pl.BlockSpec(memory_space=pltpu.SMEM), vmem, vmem]
        + [pl.BlockSpec(memory_space=pl.ANY)] * 3,
        out_specs=(vmem,) * 5,
        scratch_shapes=[
            pltpu.VMEM(latents.shape[1:], bf16),
            pltpu.VMEM(flat, jnp.float32),
            pltpu.VMEM(flat, jnp.float32),
            pltpu.VMEM(tap, bf16),
            pltpu.VMEM((9, 8, rows, width), bf16),
            pltpu.VMEM((3, images, side + 2, side, width), bf16),
            pltpu.VMEM((images, width, cells), bf16),
            pltpu.VMEM((images * cells, width), jnp.float32),
            pltpu.VMEM((9, 2, 2, 2, rows, width), bf16),
            pltpu.VMEM((9, 2, 2, rows, width), bf16),
            pltpu.VMEM((9, 2, 2, rows, width), bf16),
            pltpu.VMEM((9, 2, half, width), bf16),
            pltpu.VMEM((9, 2, rest, width), bf16),
            pltpu.VMEM((9, 2, half, width), bf16),
            pltpu.VMEM((9, 2, rest, width), bf16),
            pltpu.VMEM((9, half, width), bf16),
            pltpu.VMEM((9, rest, width), bf16),
            pltpu.VMEM((9, 3, rows, width), bf16),
            pltpu.VMEM((9, 3, rows, width), bf16),
            pltpu.VMEM(tap, bf16),
            pltpu.VMEM(tap, bf16),
            pltpu.SemaphoreType.DMA((9, 8)),
            pltpu.SemaphoreType.DMA((9, 8)),
            pltpu.SemaphoreType.DMA((9, 5)),
            pltpu.SemaphoreType.DMA((9, 5)),
            pltpu.SemaphoreType.DMA((4, 9)),
            pltpu.SemaphoreType.DMA((4, 9)),
            pltpu.SemaphoreType.DMA((3,)),
        ],
        compiler_params=pltpu.CompilerParams(
            collective_id=0, has_side_effects=True, vmem_limit_bytes=60 * 1024 * 1024
        ),
        cost_estimate=pl.CostEstimate(
            flops=6 * images * cells * 9 * width * width, bytes_accessed=16000000, transcendentals=0
        ),
    )(sources, latents[0], weights[0], cotangent[0], first_moment[0], second_moment[0])

    f32 = jnp.float32
    weights_now = jnp.where(taking, weights_in.astype(f32), weights[0])
    first_now = jnp.where(taking, first_in.astype(f32), first_moment[0])
    second_now = jnp.where(taking, second_in.astype(f32), second_moment[0])
    gradient = grad.astype(f32)
    updated, first_new, second_new = adam_update(weights_now, first_now, second_now, gradient)
    return (latent_grad[None], updated[None], first_new[None], second_new[None])


def solution(mesh):
    fits = mesh.shape["member"] == 4 and mesh.shape["dp"] == 8
    local = local_block if fits else local_plain
    in_specs = (
        P("member", "dp", None, None, None),
        P("member", "dp", None, None, None),
        P("member", "dp", None),
        P("member", "dp", None),
        P("member", "dp", None),
        P(),
    )
    out_specs = (
        P("member", "dp", None, None, None),
        P("member", "dp", None),
        P("member", "dp", None),
        P("member", "dp", None),
    )
    return jax.shard_map(local, mesh=mesh, in_specs=in_specs, out_specs=out_specs, check_vma=False)
```
